128 devices in a mesh: span: 8 (over x, y_lo), stream: 16 (over z, y_hi, core).
Axes of the slice: x: 4, y: 4 (y_hi: 2, y_lo: 2; y = y_hi * 2 + y_lo), z: 4, core: 2. Of those that a mesh axis runs over, the one named last changes fastest.
Arguments:
- adjoint: bfloat16 [3, 48, 512, 2048], P(None, 'stream', 'span'), may hold values from -6 to 6
- saved_grad: bfloat16 [9, 48, 512, 2048], P(None, 'stream', 'span'), may hold values from -4 to 4
- saved_u: bfloat16 [48, 512, 2048], P('stream', 'span'), may hold values from 0.29882812 to 1.6953125
- disk_owner: int32 [48, 512], P('stream', 'span'), may hold values from -1 to 9, as said below
- disk_weight: float32 [48, 512], P('stream', 'span'), may hold values from 0.1 to 1
- row_x: int32 [10], replicated, may hold values from 0 to 2047, as said below
- thrust: float32 [10, 10], replicated, may hold values from 0.5 to 2
- block_inverse: float32 [1024, 12, 4, 4, 256], P(('span', 'stream')), may hold values from -0.6 to 0
Outputs:
- tendency: float32 [3, 2048, 48, 512], P(None, ('span', 'stream'))
The draws below stay inside these ranges and needn't reach their ends.
Inputs may be any that keep to these rules, and one draw needn't show every extreme that they name: `disk_owner`: each turbine column c covers an elliptical disk of cells, inside the across-wind band of cells y with y * 10 // 512 = c, and at least one cell; -1 elsewhere. `row_x`: Increasing; row r lies in the cells r * (204) to (r + 1) * 204 - 1.
All inputs are finite; a program needn't handle non-finite values.
Results may differ from the reference program's by a relative error of at most 0.0003.
Values sent between devices are 32-bit elements; how exact they have to be, the bound alone decides.
No kernel may reach another device: no remote copies, remote signals or barrier semaphores. Data moves between devices by JAX's collectives and lax.ppermute only.
A program may use at most 128 MiB of HBM per device.

```python
import math
import jax
import jax.numpy as jnp
from jax import lax

NX = 2048
NY = 512
NZ = 48
ROWS = 10
COLS = 10


def draw_disk_owner(key, part):
    key = jax.random.fold_in(key, 11)
    key_center, key_hub = jax.random.split(key)
    columns = jnp.arange(COLS, dtype=jnp.int32)
    starts = columns * NY // COLS
    widths = (columns + 1) * NY // COLS - starts
    reach = max(1, NY // (COLS * 8))
    centers = starts + widths // 2 + jax.random.randint(key_center, (COLS,), -reach, reach + 1)
    centers = jnp.clip(centers, starts, starts + widths - 1)
    hub_low = NZ // 3
    hubs = jax.random.randint(key_hub, (COLS,), hub_low, hub_low + max(2, NZ // 12))
    radius_y = max(1, NY // COLS // 6)
    radius_z = max(1, NZ // 12)
    positions = jnp.arange(NY, dtype=jnp.int32)
    owner_col = positions * COLS // NY
    offset_y = (positions - centers[owner_col])[None, :] * radius_z
    levels = jnp.arange(NZ, dtype=jnp.int32)
    offset_z = (levels[:, None] - hubs[owner_col][None, :]) * radius_y
    inside = offset_y * offset_y + offset_z * offset_z <= radius_y * radius_z * (radius_y * radius_z)
    return jnp.where(inside, owner_col[None, :], -1).astype(jnp.int32)


def draw_row_x(key, part):
    key = jax.random.fold_in(key, 12)
    spacing = NX // ROWS
    offsets = jax.random.randint(key, (ROWS,), 0, spacing)
    return (jnp.arange(ROWS, dtype=jnp.int32) * spacing + offsets).astype(jnp.int32)


def draw_block_inverse(key, part):
    key = jax.random.fold_in(key, 13)
    key_diag, key_off = jax.random.split(key)
    shape = (NX // 2, NZ // 4, 4, 4, NY // 2)
    diagonal = jax.random.uniform(key_diag, shape, jnp.float32, 0.3, 0.5)
    offdiag = jax.random.uniform(key_off, shape, jnp.float32, 0.05, 0.2)
    identity = jnp.eye(4, dtype=jnp.float32)[None, None, :, :, None]
    return -(identity * diagonal + (1.0 - identity) * offdiag)


def block_scale(key, extent, shards, least, largest):
    level, own = 1.0, jax.random.fold_in(key, 6)
    for axis_at, blocks in shards:
        heights = jnp.exp(jax.random.uniform(jax.random.fold_in(own, axis_at), (blocks,), jnp.float32, least / len(shards), largest / len(shards)))
        level = level * jnp.repeat(heights, extent[axis_at] // blocks).reshape([-1 if axis == axis_at else 1 for axis in range(len(extent))])
    return level


def scatter_about(own_key, shape, deviation, most, cuts=(), kind=jnp.bfloat16):
    level = block_scale(own_key, shape, cuts, -0.22, 0.18) if cuts else 1.0
    values = jax.random.normal(own_key, shape, jnp.float32) * deviation * level
    return jnp.minimum(jnp.maximum(values, -most), most).astype(kind)


def setup_inputs(seed: int = 0) -> dict:
    keys = jax.random.split(jax.random.key(seed), 9)
    return {
        "adjoint": scatter_about(keys[0], (3, NZ, NY, NX), 1.0, 6.0, ((1, 16), (2, 8))),
        "saved_grad": scatter_about(keys[1], (9, NZ, NY, NX), 0.5, 4.0, ((1, 16), (2, 8))),
        "saved_u": jnp.clip(0.29882812 + 1.3964844 * jax.random.uniform(keys[2], (NZ, NY, NX), jnp.float32) ** block_scale(keys[2], (NZ, NY, NX), ((0, 16), (1, 8)), -0.2, 0.2), 0.29882812, 1.6953125).astype(jnp.bfloat16),
        "disk_owner": draw_disk_owner(jax.random.fold_in(keys[8], 71), 0),
        "disk_weight": jnp.clip(jnp.exp(math.log(1.0) - 2.3025851 * jax.random.uniform(keys[4], (NZ, NY), jnp.float32) ** block_scale(keys[4], (NZ, NY), ((0, 16), (1, 8)), -0.2, 0.2)), 0.1, 1.0),
        "row_x": draw_row_x(jax.random.fold_in(keys[8], 71), 0),
        "thrust": jnp.clip(jnp.exp(jax.random.uniform(keys[6], (ROWS, COLS), jnp.float32, math.log(0.5), math.log(2.0))), 0.5, 2.0),
        "block_inverse": draw_block_inverse(jax.random.fold_in(keys[8], 71), 0),
    }


def derive_x(operand, wavenumber):
    scale = wavenumber[:, None, None, None]
    cosine = operand[..., :, 0, :, :, :]
    sine = operand[..., :, 1, :, :, :]
    return jnp.stack([scale * sine, -scale * cosine], axis=-4)

def derive_y(operand, wavenumber):
    cosine = operand[..., 0, :]
    sine = operand[..., 1, :]
    return jnp.stack([wavenumber * sine, -wavenumber * cosine], axis=-2)

def derive_z(operand):
    padded = jnp.pad(operand, ((0, 0), (0, 0), (1, 1), (0, 0), (0, 0)))
    return 0.5 * (padded[:, :, 2:] - padded[:, :, :-2])

def solve_levels(right_side, inverses):
    modes, _, levels, _, halves = right_side.shape
    blocks = levels // 4
    grouped = right_side.reshape(modes, 2, blocks, 4, 2, halves).transpose(2, 3, 0, 1, 4, 5)
    matrices = inverses.transpose(1, 2, 3, 0, 4)[:, :, :, :, None, None, :]

    def forward(running, pieces):
        segment, inverse_block = pieces
        first = segment[0] - running
        segment = jnp.concatenate([first[None], segment[1:]], axis=0)
        solved = lax.optimization_barrier(jnp.sum(inverse_block * segment[None], axis=1))
        return (solved[3], solved)
    start = jnp.zeros((modes, 2, 2, halves), jnp.float32)
    _, partial_out = lax.scan(forward, start, (grouped, matrices))

    def backward(running, pieces):
        solved, inverse_block = pieces
        result = solved - inverse_block[:, 3] * running[None]
        return (result[0], result)
    _, levels_out = lax.scan(backward, start, (partial_out, matrices), reverse=True)
    return levels_out.transpose(2, 3, 0, 1, 4, 5).reshape(modes, 2, levels, 2, halves)

def project(spectrum, inverses, along_wind, across_wind):
    modes = along_wind.shape[0]
    halves = across_wind.shape[0]
    levels = spectrum.shape[2]
    parts = spectrum.reshape(3, modes, 2, levels, 2, halves)
    divergence = derive_x(parts[0], along_wind) + derive_y(parts[1], across_wind) + derive_z(parts[2])
    pressure = solve_levels(divergence, inverses)
    gradient = jnp.stack([derive_x(pressure, along_wind), derive_y(pressure, across_wind), derive_z(pressure)])
    return (parts - gradient).reshape(spectrum.shape)

def reference(adjoint, saved_grad, saved_u, disk_owner, disk_weight, row_x, thrust, block_inverse):
    exact_mode = lax.Precision.HIGHEST
    adjoint_wide = adjoint.astype(jnp.float32)
    coupling = jnp.stack([sum((adjoint_wide[partner] * saved_grad[3 * component + partner].astype(jnp.float32) for partner in range(3))) for component in range(3)])
    columns = jnp.arange(COLS, dtype=jnp.int32)
    weighted = jnp.where(disk_owner[:, :, None] == columns[None, None, :], disk_weight[:, :, None], 0.0)
    column_speed = jnp.take(saved_u, row_x, axis=2).astype(jnp.float32)
    column_adjoint = jnp.take(adjoint[0], row_x, axis=2).astype(jnp.float32)
    speed_sum = jnp.einsum('zyr,zyc->rc', column_speed, weighted, precision=exact_mode)
    adjoint_sum = jnp.einsum('zyr,zyc->rc', column_adjoint, weighted, precision=exact_mode)
    disk_area = lax.optimization_barrier(jnp.sum(weighted, axis=(0, 1)))
    disk_speed = speed_sum / disk_area
    disk_adjoint = adjoint_sum / disk_area
    disk_coeff = -thrust * disk_speed * (1.5 * disk_speed + disk_adjoint)
    cell_term = jnp.einsum('zyc,rc->zyr', weighted, disk_coeff, precision=exact_mode)
    placement = (jnp.arange(NX, dtype=jnp.int32)[None, :] == row_x[:, None]).astype(jnp.float32)
    extra = jnp.einsum('zyr,rx->zyx', cell_term, placement, precision=exact_mode)
    source = jnp.concatenate([(coupling[0] + extra)[None], coupling[1:]], axis=0)
    along = jnp.fft.rfft(source, axis=-1)[..., :NX // 2]
    cosine = (along.real / math.sqrt(NX)).astype(jnp.float32)
    sine = (-along.imag / math.sqrt(NX)).astype(jnp.float32)
    paired = jnp.stack([cosine, sine], axis=-1).reshape(3, NZ, NY, NX).transpose(0, 3, 1, 2)
    across = jnp.fft.rfft(paired, axis=-1)[..., :NY // 2]
    spectrum = (jnp.concatenate([across.real, -across.imag], axis=-1) / math.sqrt(NY)).astype(jnp.float32)
    along_wind = 2.0 * math.pi * jnp.arange(NX // 2, dtype=jnp.float32) / NX
    across_wind = 2.0 * math.pi * jnp.arange(NY // 2, dtype=jnp.float32) / NY
    return project(spectrum, block_inverse, along_wind, across_wind)
```

```python
import functools
import math

import jax
import jax.numpy as jnp
import ml_dtypes
import numpy as np
from jax import lax
from jax.experimental import pallas as pl
from jax.experimental.pallas import tpu as pltpu
from jax.sharding import PartitionSpec as P

NX = 2048
NY = 512
NZ = 48
ROWS = 10
COLS = 10
HALF = NX // 2
BLOCKS = NZ // 4
WIDE = 1280
CHUNK = 256
F32 = jnp.float32
BF16 = jnp.bfloat16
VMEM_BYTES = 56 * 1024 * 1024


def split_table(values):
    high = values.astype(ml_dtypes.bfloat16)
    low = (values - high.astype(np.float64)).astype(ml_dtypes.bfloat16)
    return high, low


@functools.lru_cache(maxsize=None)
def along_tables():
    row = np.arange(HALF)
    out = []
    for parity in range(2):
        mode = 8 * (row // 8) + 2 * (row % 4) + parity
        sine = (row // 4) % 2
        phase = mode[:, None] * np.arange(HALF)[None, :] % NX
        angle = phase * (2.0 * np.pi / NX)
        out.append(np.where(sine[:, None] == 0, np.cos(angle), np.sin(angle)) / np.sqrt(NX))
    return split_table(np.stack(out))


@functools.lru_cache(maxsize=None)
def across_tables():
    basis = np.arange(NY)
    phase = np.arange(NY)[:, None] * (basis % (NY // 2))[None, :] % NY
    angle = phase * (2.0 * np.pi / NY)
    values = np.where((basis // (NY // 2))[None, :] == 0, np.cos(angle), np.sin(angle))
    return split_table(values / np.sqrt(NY))


def split(value):
    high = value.astype(BF16)
    return high, (value - high.astype(F32)).astype(BF16)


def dot_nt(left, right):
    return lax.dot_general(left, right, (((1,), (1,)), ((), ())), preferred_element_type=F32)


def dot_nn(left, right):
    return jnp.dot(left, right, preferred_element_type=F32)


def along_kernel(
    row_x, first_column, adjoint, grad, saved_u, owner, weight, table_high, table_low,
    out, source_high, source_low, tail_high, tail_low, onehot, extra,
):
    step = pl.program_id(0)

    @pl.when(step == 0)
    def _():
        lane = lax.broadcasted_iota(jnp.int32, (1, 128), 1)
        wanted = jnp.full((1, 128), -1, jnp.int32)
        for r in range(ROWS):
            wanted = jnp.where(lane == r, row_x[r], wanted)
        cell = lax.broadcasted_iota(jnp.int32, (NX, 128), 0)
        onehot[...] = jnp.where(cell == wanted, 1.0, 0.0).astype(BF16)
        extra[...] = jnp.zeros((8, 128), F32)
        tail_high[...] = jnp.zeros(tail_high.shape, BF16)
        tail_low[...] = jnp.zeros(tail_low.shape, BF16)

    for level in range(3):

        @pl.when(step == level)
        def _(level=level):
            velocity = [adjoint[j, 0].astype(F32) for j in range(3)]
            for i in range(3):
                value = velocity[0] * grad[3 * i, 0].astype(F32)
                for j in range(1, 3):
                    value = value + velocity[j] * grad[3 * i + j, 0].astype(F32)
                left, right = value[:, :HALF], value[:, HALF:]
                pair = 3 * i + level
                for parity, folded in enumerate((left + right, left - right)):
                    high, low = split(folded)
                    if pair < 8:
                        source_high[parity, pl.ds(64 * pair, 64)] = high
                        source_low[parity, pl.ds(64 * pair, 64)] = low
                    else:
                        tail_high[parity, pl.ds(64 * parity, 64)] = high
                        tail_low[parity, pl.ds(64 * parity, 64)] = low
            column_u = dot_nn(saved_u[0], onehot[...])
            column_a = dot_nn(adjoint[0, 0], onehot[...])
            lane = lax.broadcasted_iota(jnp.int32, (64, 128), 1)
            column_u = jnp.where(lane == ROWS, 1.0, column_u).astype(BF16)
            column_a = column_a.astype(BF16)
            own = owner[level : level + 1, :]
            heavy = weight[level : level + 1, :]
            masked = jnp.where(own >= 0, heavy, 0.0)
            row = lax.broadcasted_iota(jnp.int32, (8, 64), 0)
            rest = jnp.where(own == first_column[0] + row % 2, heavy, 0.0)
            sum_u = jnp.zeros((8, 128), F32)
            sum_a = jnp.zeros((8, 128), F32)
            for _ in range(3):
                part = rest.astype(BF16)
                rest = rest - part.astype(F32)
                sum_u = sum_u + dot_nn(part, column_u)
                sum_a = sum_a + dot_nn(part, column_a)
            row = lax.broadcasted_iota(jnp.int32, (8, 128), 0)
            added = jnp.where(row < 2, sum_u, jnp.where(row < 4, sum_a, 0.0))
            padded = jnp.concatenate([masked, jnp.zeros((1, 64), F32)], axis=1)
            extra[...] += jnp.where(row == 4 + level, padded, added)

    @pl.when(step >= 3)
    def _():
        dests = CHUNK // 8
        tail = jnp.zeros((CHUNK, 128), F32)
        for parity in range(2):
            high, low = table_high[parity], table_low[parity]
            body = dot_nt(high, source_high[parity])
            body = body + dot_nt(high, source_low[parity])
            body = body + dot_nt(low, source_high[parity])
            out[:, :, 512 * parity : 512 * parity + 512] = body.reshape(dests, 8, 512)
            tail = tail + dot_nt(high, tail_high[parity])
            tail = tail + dot_nt(high, tail_low[parity])
            tail = tail + dot_nt(low, tail_high[parity])
        out[:, :, 1024:1152] = tail.reshape(dests, 8, 128)
        out[:, :, 1152:1280] = jnp.broadcast_to(extra[...][None], (dests, 8, 128))


def along(adjoint, grad, saved_u, owner, weight, row_x, first_column):
    table_high, table_low = along_tables()
    chunks = HALF // CHUNK

    def level_of(step):
        return jnp.minimum(step, 2)

    def chunk_of(step):
        return jnp.maximum(step - 3, 0)

    return pl.pallas_call(
        along_kernel,
        grid=(3 + chunks,),
        out_shape=jax.ShapeDtypeStruct((128, 8, WIDE), F32),
        in_specs=[
            pl.BlockSpec(memory_space=pltpu.SMEM),
            pl.BlockSpec(memory_space=pltpu.SMEM),
            pl.BlockSpec((3, 1, 64, NX), lambda s: (0, level_of(s), 0, 0)),
            pl.BlockSpec((9, 1, 64, NX), lambda s: (0, level_of(s), 0, 0)),
            pl.BlockSpec((1, 64, NX), lambda s: (level_of(s), 0, 0)),
            pl.BlockSpec((3, 64), lambda s: (0, 0)),
            pl.BlockSpec((3, 64), lambda s: (0, 0)),
            pl.BlockSpec((2, CHUNK, HALF), lambda s: (0, chunk_of(s), 0)),
            pl.BlockSpec((2, CHUNK, HALF), lambda s: (0, chunk_of(s), 0)),
        ],
        out_specs=pl.BlockSpec((CHUNK // 8, 8, WIDE), lambda s: (chunk_of(s), 0, 0)),
        scratch_shapes=[
            pltpu.VMEM((2, 512, HALF), BF16),
            pltpu.VMEM((2, 512, HALF), BF16),
            pltpu.VMEM((2, 128, HALF), BF16),
            pltpu.VMEM((2, 128, HALF), BF16),
            pltpu.VMEM((NX, 128), BF16),
            pltpu.VMEM((8, 128), F32),
        ],
        compiler_params=pltpu.CompilerParams(vmem_limit_bytes=VMEM_BYTES),
        name="along",
    )(row_x, first_column, adjoint, grad, saved_u, owner, weight,
      jnp.asarray(table_high), jnp.asarray(table_low))


def signed_x(value, scale):
    return jnp.concatenate(
        [scale[c] * pltpu.roll(value[8 * c : 8 * c + 8], 4, 0) for c in range(2)], axis=0
    )


def signed_y(value, scale):
    return jnp.concatenate([scale * value[:, 256:], -scale * value[:, :256]], axis=1)


def across_kernel(
    received, extras, thrust, row_basis, wave_x, wave_y, inverses, table_high, table_low,
    out, spectrum, solved, grid_high, grid_low, forced, heavy, above,
):
    step = pl.program_id(0)
    low_half = lax.broadcasted_iota(jnp.int32, (1, 1, 128), 2) < 64

    @pl.when(step == 0)
    def _():
        all_extras = extras[...].reshape(8, 16, 8, 128)
        total = jnp.sum(all_extras, axis=1)
        column = lax.broadcasted_iota(jnp.int32, (16, 128), 0)
        sum_u = jnp.zeros((16, 128), F32)
        sum_a = jnp.zeros((16, 128), F32)
        for s in range(8):
            for other in range(2):
                hit = column == 5 * s // 4 + other
                sum_u = sum_u + jnp.where(hit, total[s, other : other + 1, :], 0.0)
                sum_a = sum_a + jnp.where(hit, total[s, 2 + other : 3 + other, :], 0.0)
        lane = lax.broadcasted_iota(jnp.int32, (16, 128), 1)
        valid = (lane < ROWS) & (column < COLS)
        area = jnp.where(valid, sum_u[:, ROWS : ROWS + 1], 1.0)
        speed = sum_u / area
        reverse = sum_a / area
        coeff = jnp.where(valid, -thrust[...] * speed * (1.5 * speed + reverse), 0.0)
        cell = lax.broadcasted_iota(jnp.int32, (16, NY), 1)
        band = lax.broadcasted_iota(jnp.int32, (16, NY), 0)
        spread = jnp.where(cell * COLS // NY == band, 1.0, 0.0).astype(F32)
        exact = lax.Precision.HIGHEST
        per_column = lax.dot_general(
            row_basis[...], coeff, (((1,), (1,)), ((), ())), precision=exact,
            preferred_element_type=F32,
        )
        forced[...] = jnp.dot(per_column, spread, precision=exact, preferred_element_type=F32)
        for j in range(4):
            left = all_extras[2 * j]
            right = pltpu.roll(all_extras[2 * j + 1], 64, 2)
            heavy[:, :, 128 * j : 128 * j + 128] = jnp.where(low_half, left, right)

    @pl.when(step < 4)
    def _():
        for tile in range(9):
            lanes = pl.ds(128 * tile, 128)
            for j in range(4):
                left = received[2 * j, :, :, lanes]
                right = received[2 * j + 1, :, :, lanes]
                values = (
                    jnp.where(low_half, left, pltpu.roll(right, 64, 2)),
                    jnp.where(low_half, pltpu.roll(left, 64, 2), right),
                )
                for side in range(2):
                    if tile < 8:
                        parity, pair = tile // 4, 2 * (tile % 4) + side
                    else:
                        parity, pair = side, 8
                    component, inner = pair // 3, pair % 3
                    value = values[side]
                    cells = slice(128 * j, 128 * j + 128)
                    if component == 0:
                        disk = heavy[pl.ds(4 * step, 4), 4 + inner : 5 + inner, cells]
                        value = value + disk * forced[8 * parity : 8 * parity + 8, cells][None]
                    for t in range(4):
                        spectrum[component, 12 * step + 3 * t + inner, 8 * parity : 8 * parity + 8, cells] = value[t]
        for component in range(3):
            high, low = split(spectrum[component, pl.ds(12 * step, 12)].reshape(192, NY))
            grid_high[pl.ds(192 * component, 192)] = high
            grid_low[pl.ds(192 * component, 192)] = low
        result = dot_nn(grid_high[...], table_high[...])
        result = result + dot_nn(grid_low[...], table_high[...])
        result = result + dot_nn(grid_high[...], table_low[...])
        spectrum[:, pl.ds(12 * step, 12)] = result.reshape(3, 12, 16, NY)

    scale_x = [wave_x[c] for c in range(2)]
    scale_y = wave_y[0:1, :]

    def forward(block, carry):
        entries = []
        for i in range(4):
            z = 4 * block + i
            up = spectrum[2, jnp.minimum(z + 1, NZ - 1)]
            up = jnp.where(z + 1 < NZ, up, 0.0)
            down = spectrum[2, jnp.maximum(z - 1, 0)]
            down = jnp.where(z > 0, down, 0.0)
            entries.append(
                signed_x(spectrum[0, z], scale_x)
                + signed_y(spectrum[1, z], scale_y)
                + 0.5 * (up - down)
            )
        entries[0] = entries[0] - carry
        last = None
        for i in range(4):
            halves = []
            for q in range(2):
                total = inverses[block, 4 * i] * entries[0][:, 256 * q : 256 * q + 256]
                for j in range(1, 4):
                    total = total + inverses[block, 4 * i + j] * entries[j][:, 256 * q : 256 * q + 256]
                halves.append(total)
            last = jnp.concatenate(halves, axis=1)
            solved[4 * block + i] = last
        return last

    @pl.when(step == 3)
    def _():
        lax.fori_loop(0, BLOCKS, forward, jnp.zeros((16, NY), F32))
        above[...] = jnp.zeros((16, NY), F32)

    def corrected(block, i, running):
        column = inverses[block, 4 * i + 3]
        return solved[4 * block + i] - jnp.concatenate([column, column], axis=1) * running

    @pl.when(step >= 4)
    def _():
        group = 9 - step
        first = 2 * group
        upper = above[...]
        running = upper
        pressure = [None] * 8
        for half in (1, 0):
            for i in range(4):
                pressure[4 * half + i] = corrected(first + half, i, running)
            running = pressure[4 * half]
        before = corrected(jnp.maximum(first - 1, 0), 3, running)
        before = jnp.where(group > 0, before, 0.0)
        above[...] = running
        pressure = [before] + pressure + [upper]
        for component in range(3):
            rows = []
            for z in range(8):
                here = pressure[z + 1]
                if component == 0:
                    slope = signed_x(here, scale_x)
                elif component == 1:
                    slope = signed_y(here, scale_y)
                else:
                    slope = 0.5 * (pressure[z + 2] - pressure[z])
                rows.append(spectrum[component, 8 * group + z] - slope)
            for m in range(16):
                source = 8 * ((m // 2) % 2) + 4 * (m % 2) + m // 4
                out[component, m] = jnp.concatenate(
                    [rows[z][source : source + 1] for z in range(8)], axis=0
                )


def across(received, thrust, row_basis, wave_x, wave_y, inverses):
    table_high, table_low = across_tables()

    def whole(shape):
        return pl.BlockSpec(shape, lambda s: (0,) * len(shape))

    return pl.pallas_call(
        across_kernel,
        grid=(10,),
        out_shape=jax.ShapeDtypeStruct((3, 16, NZ, NY), F32),
        in_specs=[
            pl.BlockSpec((8, 4, 8, WIDE), lambda s: (0, jnp.minimum(s, 3), 0, 0)),
            pl.BlockSpec((8, 16, 8, 128), lambda s: (0, 0, 0, 9)),
            whole((16, 128)),
            whole((16, 128)),
            whole((2, 8, 1)),
            whole((1, 256)),
            whole((BLOCKS, 16, 16, 256)),
            whole((NY, NY)),
            whole((NY, NY)),
        ],
        out_specs=pl.BlockSpec((3, 16, 8, NY), lambda s: (0, 0, jnp.minimum(9 - s, 5), 0)),
        scratch_shapes=[
            pltpu.VMEM((3, NZ, 16, NY), F32),
            pltpu.VMEM((NZ, 16, NY), F32),
            pltpu.VMEM((576, NY), BF16),
            pltpu.VMEM((576, NY), BF16),
            pltpu.VMEM((16, NY), F32),
            pltpu.VMEM((16, 8, NY), F32),
            pltpu.VMEM((16, NY), F32),
        ],
        compiler_params=pltpu.CompilerParams(vmem_limit_bytes=VMEM_BYTES),
        name="across",
    )(received, received, thrust, row_basis, wave_x, wave_y, inverses,
      jnp.asarray(table_high), jnp.asarray(table_low))


def body(adjoint, saved_grad, saved_u, disk_owner, disk_weight, row_x, thrust, block_inverse):
    axes = ("span", "stream")
    span = lax.axis_index("span")
    first_column = (5 * span // 4).astype(jnp.int32).reshape(1)
    sent = along(adjoint, saved_grad, saved_u, disk_owner, disk_weight, row_x, first_column)
    received = lax.all_to_all(sent, axes, split_axis=0, concat_axis=0, tiled=True)

    first_mode = lax.axis_index(axes) * 8
    row = jnp.arange(16, dtype=jnp.int32)
    mode = first_mode + 2 * (row % 4) + row // 8
    sine = (row // 4) % 2
    wave = 2.0 * math.pi * mode.astype(F32) / NX
    wave_x = jnp.where(sine == 0, wave, -wave).reshape(2, 8, 1)
    wave_y = (2.0 * math.pi * jnp.arange(NY // 2, dtype=F32) / NY).reshape(1, 256)
    angle = (mode[:, None] * row_x[None, :] % NX).astype(F32) * (2.0 * math.pi / NX)
    basis = jnp.where(sine[:, None] == 0, jnp.cos(angle), jnp.sin(angle)) / math.sqrt(NX)
    row_basis = jnp.pad(basis, ((0, 0), (0, 128 - ROWS)))
    thrust_t = jnp.pad(thrust.T, ((0, 16 - COLS), (0, 128 - ROWS)))
    folded = block_inverse.reshape(4, 2, BLOCKS, 16, 256).transpose(2, 3, 1, 0, 4)
    inverses = jnp.broadcast_to(
        folded[:, :, :, None], (BLOCKS, 16, 2, 2, 4, 256)
    ).reshape(BLOCKS, 16, 16, 256)
    return across(
        received.reshape(8, 16, 8, WIDE), thrust_t, row_basis, wave_x, wave_y, inverses
    )


def solution(mesh):
    in_specs = (
        P(None, "stream", "span", None),
        P(None, "stream", "span", None),
        P("stream", "span", None),
        P("stream", "span"),
        P("stream", "span"),
        P(),
        P(),
        P(("span", "stream"), None, None, None, None),
    )
    out_specs = P(None, ("span", "stream"), None, None)
    return jax.shard_map(body, mesh=mesh, in_specs=in_specs, out_specs=out_specs, check_vma=False)
```

```python
import functools
import math

import jax
import jax.numpy as jnp
import ml_dtypes
import numpy as np
from jax import lax
from jax.experimental import pallas as pl
from jax.experimental.pallas import tpu as pltpu
from jax.sharding import PartitionSpec as P

NX = 2048
NY = 512
NZ = 48
ROWS = 10
COLS = 10
HALF = NX // 2
BLOCKS = NZ // 4
DESTS = 128
ROWS_SENT = 74
GROUP = 4 * ROWS_SENT
F32 = jnp.float32
BF16 = jnp.bfloat16
VMEM_BYTES = 58 * 1024 * 1024


def split_table(values):
    high = values.astype(ml_dtypes.bfloat16)
    low = (values - high.astype(np.float64)).astype(ml_dtypes.bfloat16)
    return high, low


def wave_rows(mode, sine, length):
    phase = mode[:, None] * np.arange(length)[None, :] % NX
    angle = phase * (2.0 * np.pi / NX)
    return np.where(sine[:, None] == 0, np.cos(angle), np.sin(angle)) / np.sqrt(NX)


@functools.lru_cache(maxsize=None)
def along_tables():
    row = np.arange(HALF)
    sine, rest = (row // 4) % 2, row % 4
    odd = wave_rows(8 * (row // 8) + 2 * rest + 1, sine, HALF)
    row = np.arange(HALF // 2)
    sine, slot, inner = (row // 4) % 2, (row // 2) % 2, row % 2
    even = [
        wave_rows(8 * (2 * (row // 8) + (slot ^ kind)) + 4 * inner + 2 * kind, sine, HALF // 2)
        for kind in range(2)
    ]
    return np.stack(split_table(odd)), np.stack(split_table(np.stack(even)))


@functools.lru_cache(maxsize=None)
def across_tables():
    basis = np.arange(NY)
    phase = np.arange(NY)[:, None] * (basis % (NY // 2))[None, :] % NY
    angle = phase * (2.0 * np.pi / NY)
    values = np.where((basis // (NY // 2))[None, :] == 0, np.cos(angle), np.sin(angle))
    return np.stack(split_table(values / np.sqrt(NY)))


def split(value):
    high = value.astype(BF16)
    return high, (value - high.astype(F32)).astype(BF16)


def dot_nt(left, right):
    return lax.dot_general(left, right, (((1,), (1,)), ((), ())), preferred_element_type=F32)


def dot_nn(left, right):
    return jnp.dot(left, right, preferred_element_type=F32)


def couple(level, steps, adjoint, grad, highs, lows, tail):
    quarter = NX // 4
    for step in steps:
        rows = pl.ds(pl.multiple_of(16 * step, 16), 16)
        for start in range(0, quarter, 128):
            lanes = [pl.ds(quarter * n + start, 128) for n in range(4)]
            velocity = [[adjoint[j, level, rows, l].astype(F32) for l in lanes] for j in range(3)]
            for i in range(3):
                value = []
                for n, l in enumerate(lanes):
                    total = velocity[0][n] * grad[3 * i, level, rows, l].astype(F32)
                    for j in range(1, 3):
                        total = total + velocity[j][n] * grad[3 * i + j, level, rows, l].astype(F32)
                    value.append(total)
                first, second = value[0] + value[2], value[1] + value[3]
                folded = (value[0] - value[2], value[1] - value[3], first + second, first - second)
                pair = 3 * level + i
                window, place = pair // 4, 64 * (pair % 4)
                for n in range(4):
                    high, low = split(folded[n])
                    target = pl.ds(pl.multiple_of(place + 16 * step, 16), 16)
                    if window < 2:
                        highs[window][target, lanes[n]] = high
                        lows[window][target, lanes[n]] = low
                    else:
                        tail[target, lanes[n]] = high
                        tail[pl.ds(pl.multiple_of(64 + 16 * step, 16), 16), lanes[n]] = low


def along_kernel(
    row_x, first_column, owner, weight, adjoint_hbm, grad_hbm, saved_u_hbm, odd_hbm, even_hbm,
    out, adjoint, grad, saved_u, odd, even, high_0, high_1, low_0, low_1, tail, onehot, outbox, sems,
):
    highs, lows = (high_0, high_1), (low_0, low_1)
    copies = []
    for level in range(3):
        copies.append(pltpu.make_async_copy(adjoint_hbm.at[:, level], adjoint.at[:, level], sems.at[2 * level]))
        copies.append(pltpu.make_async_copy(grad_hbm.at[:, level], grad.at[:, level], sems.at[2 * level + 1]))
    fetch_u = pltpu.make_async_copy(saved_u_hbm, saved_u, sems.at[6])
    fetch_odd = pltpu.make_async_copy(odd_hbm, odd, sems.at[7])
    fetch_even = pltpu.make_async_copy(even_hbm, even, sems.at[8])
    for copy in copies[:4] + [fetch_u] + copies[4:] + [fetch_odd, fetch_even]:
        copy.start()

    lane = lax.broadcasted_iota(jnp.int32, (1, 128), 1) % 16
    wanted = jnp.full((1, 128), -1, jnp.int32)
    for r in range(ROWS):
        wanted = jnp.where(lane == r, row_x[r], wanted)

    def mark(step, _):
        rows = pl.ds(pl.multiple_of(256 * step, 256), 256)
        cell = lax.broadcasted_iota(jnp.int32, (256, 128), 0) + 256 * step
        onehot[rows, :] = jnp.where(cell == wanted, 1.0, 0.0).astype(BF16)
        return 0

    lax.fori_loop(0, NX // 256, mark, 0)

    def couple_rows(level):
        def rows_of(step, _):
            couple(level, (step,), adjoint, grad, highs, lows, tail)
            return 0

        lax.fori_loop(0, 4, rows_of, 0)

    for level in range(3):
        copies[2 * level].wait()
        copies[2 * level + 1].wait()
        if level < 2:
            couple_rows(level)

    fetch_u.wait()
    sum_u = jnp.zeros((8, 128), F32)
    sum_a = jnp.zeros((8, 128), F32)
    masked = []
    for level in range(3):
        column_u = dot_nn(saved_u[level], onehot[...])
        column_a = dot_nn(adjoint[0, level], onehot[...]).astype(BF16)
        column_u = jnp.where(lane == ROWS, 1.0, column_u).astype(BF16)
        own = owner[level : level + 1, :]
        heavy = weight[level : level + 1, :]
        masked.append(jnp.where(own >= 0, heavy, 0.0))
        row = lax.broadcasted_iota(jnp.int32, (8, 64), 0)
        rest = jnp.where(own == first_column[0] + row % 2, heavy, 0.0)
        for _ in range(3):
            part = rest.astype(BF16)
            rest = rest - part.astype(F32)
            sum_u = sum_u + dot_nn(part, column_u)
            sum_a = sum_a + dot_nn(part, column_a)
    place = lax.broadcasted_iota(jnp.int32, (1, 128), 1) // 16
    sums = jnp.where(place == 4, sum_u[0:1], sum_u[1:2])
    sums = jnp.where(place == 6, sum_a[0:1], jnp.where(place == 7, sum_a[1:2], sums))
    last = jnp.concatenate([masked[2], jnp.zeros((1, 64), F32)], axis=1)
    last = jnp.where(place < 4, last, sums)
    extra = jnp.concatenate([jnp.concatenate(masked[:2], axis=1), last], axis=0)

    fetch_odd.wait()
    fetch_even.wait()
    first_slot = lax.broadcasted_iota(jnp.int32, (8, 128), 0) % 4 < 2
    low_half = lax.broadcasted_iota(jnp.int32, (8, 128), 1) < 64
    spans = (pl.ds(0, HALF), pl.ds(HALF, HALF // 2), pl.ds(HALF + HALF // 2, HALF // 2))

    def tables_of(step):
        odd_rows = pl.ds(pl.multiple_of(512 * step, 512), 512)
        even_rows = pl.ds(pl.multiple_of(256 * step, 256), 256)
        return [
            [odd[n, odd_rows, :] for n in range(2)],
            [even[n, 0, even_rows, :] for n in range(2)],
            [even[n, 1, even_rows, :] for n in range(2)],
        ]

    def store(step, dest, tile, value):
        start = ROWS_SENT * (dest % 4) + 8 * tile
        outbox[16 * step + dest // 4, pl.ds(start, 8), :] = value

    def pick(dest, products):
        pair = slice(8 * (dest // 2), 8 * (dest // 2) + 8)
        kinds = (products[1][pair], products[2][pair])
        even_part = jnp.where(first_slot, kinds[dest % 2], kinds[1 - dest % 2])
        return even_part, products[0][8 * dest : 8 * dest + 8]

    def main_part(step, window):
        products = []
        for (high, low), span in zip(tables_of(step), spans):
            body = dot_nt(high, highs[window][:, span])
            body = body + dot_nt(high, lows[window][:, span])
            products.append(body + dot_nt(low, highs[window][:, span]))
        for half in range(2):
            part = [p[:, 128 * half : 128 * half + 128] for p in products]
            for dest in range(64):
                even_part, odd_part = pick(dest, part)
                store(step, dest, 2 * window + half, even_part)
                store(step, dest, 4 + 2 * window + half, odd_part)

    def first(step, _):
        couple(2, (2 * step, 2 * step + 1), adjoint, grad, highs, lows, tail)
        main_part(step, 0)
        return 0

    lax.fori_loop(0, 2, first, 0)

    def send(step):
        part = pl.ds(16 * step, 16)
        return pltpu.make_async_copy(outbox.at[part], out.at[part], sems.at[9 + step])

    def second(step, _):
        products = []
        for (high, low), span in zip(tables_of(step), spans):
            body = dot_nt(high, tail[:, span]) + dot_nt(low, tail[:, span])
            products.append(body + pltpu.roll(body, 64, 1))
        for dest in range(64):
            even_part, odd_part = pick(dest, products)
            store(step, dest, 8, jnp.where(low_half, even_part, odd_part))
            outbox[16 * step + dest // 4, pl.ds(ROWS_SENT * (dest % 4) + 72, 2), :] = extra
        main_part(step, 1)
        send(step).start()
        return 0

    lax.fori_loop(0, 2, second, 0)
    send(0).wait()
    send(1).wait()


def along(adjoint, grad, saved_u, owner, weight, row_x, first_column):
    odd, even = along_tables()
    smem = pl.BlockSpec(memory_space=pltpu.SMEM)
    vmem = pl.BlockSpec(memory_space=pltpu.VMEM)
    hbm = pl.BlockSpec(memory_space=pltpu.HBM)
    return pl.pallas_call(
        along_kernel,
        out_shape=jax.ShapeDtypeStruct((DESTS // 4, GROUP, 128), F32),
        in_specs=[smem, smem, vmem, vmem, hbm, hbm, hbm, hbm, hbm],
        out_specs=hbm,
        scratch_shapes=[
            pltpu.VMEM((3, 3, 64, NX), BF16),
            pltpu.VMEM((9, 3, 64, NX), BF16),
            pltpu.VMEM((3, 64, NX), BF16),
            pltpu.VMEM(odd.shape, BF16),
            pltpu.VMEM(even.shape, BF16),
            pltpu.VMEM((256, NX), BF16),
            pltpu.VMEM((256, NX), BF16),
            pltpu.VMEM((256, NX), BF16),
            pltpu.VMEM((256, NX), BF16),
            pltpu.VMEM((128, NX), BF16),
            pltpu.VMEM((NX, 128), BF16),
            pltpu.VMEM((DESTS // 4, GROUP, 128), F32),
            pltpu.SemaphoreType.DMA((11,)),
        ],
        compiler_params=pltpu.CompilerParams(vmem_limit_bytes=VMEM_BYTES),
        name="along",
    )(row_x, first_column, owner, weight, adjoint, grad, saved_u, jnp.asarray(odd), jnp.asarray(even))


def signed_x(value, scale):
    return jnp.concatenate(
        [scale[c] * pltpu.roll(value[8 * c : 8 * c + 8], 4, 0) for c in range(2)], axis=0
    )


def signed_y(value, scale):
    return jnp.concatenate([scale * value[:, 256:], -scale * value[:, :256]], axis=1)


def across_kernel(
    parity, thrust, row_basis, wave_x, wave_y, received_hbm, inverses_hbm, tables_hbm,
    out, received, inverses, tables, spectrum, solved, grid_high, grid_low, forced, heavy, staged, sems,
):
    fetch = []
    for group in range(4):
        for s in range(8):
            fetch.append(pltpu.make_async_copy(
                received_hbm.at[4 * s + group], received.at[4 * s + group], sems.at[6 + group]
            ))
    fetch_tables = pltpu.make_async_copy(tables_hbm, tables, sems.at[10])
    fetch_inverses = pltpu.make_async_copy(inverses_hbm, inverses, sems.at[11])
    for copy in fetch[:8] + [fetch_tables] + fetch[8:] + [fetch_inverses]:
        copy.start()
    low_half = lax.broadcasted_iota(jnp.int32, (1, 128), 1) < 64
    low_half3 = low_half[None]

    def place(group, t, component):
        for tile in range(9):
            rows = pl.ds(ROWS_SENT * t + 8 * tile, 8)
            for side in range(2):
                kind, pair = (tile // 4, 2 * (tile % 4) + side) if tile < 8 else (side, 8)
                if pair % 3 != component:
                    continue
                inner = pair // 3
                for j in range(4):
                    cells = pl.ds(128 * j, 128)
                    left = received[8 * j + group, rows, :]
                    right = received[8 * j + 4 + group, rows, :]
                    if side == 0:
                        value = jnp.where(low_half, left, pltpu.roll(right, 64, 1))
                    else:
                        value = jnp.where(low_half, pltpu.roll(left, 64, 1), right)
                    if component == 0:
                        disk = heavy[inner, t, group, :, cells]
                        value = value + disk * forced[pl.ds(8 * kind, 8), cells]
                    spectrum[component, 12 * group + 3 * t + inner, pl.ds(8 * kind, 8), cells] = value

    def multiply(parts):
        for n, (component, group) in enumerate(parts):
            high, low = split(spectrum[component, pl.ds(12 * group, 12)].reshape(192, NY))
            grid_high[pl.ds(192 * n, 192)] = high
            grid_low[pl.ds(192 * n, 192)] = low
        result = dot_nn(grid_high[...], tables[0])
        result = result + dot_nn(grid_low[...], tables[0])
        result = result + dot_nn(grid_high[...], tables[1])
        for n, (component, group) in enumerate(parts):
            spectrum[component, pl.ds(12 * group, 12)] = result[192 * n : 192 * n + 192].reshape(12, 16, NY)

    for group in range(4):
        for copy in fetch[8 * group : 8 * group + 8]:
            copy.wait()
        if group == 0:
            fetch_tables.wait()

        for t in range(4):
            place(group, t, 1)
            place(group, t, 2)
        multiply(((1, group), (2, group)))

    total = jnp.zeros((8, 1, 128), F32)
    for t in range(4):
        start = ROWS_SENT * t + 72
        upper = received[:, pl.ds(start, 1), :].reshape(4, 2, 4, 1, 128)
        lower = received[:, pl.ds(start + 1, 1), :]
        total = total + jnp.sum(lower.reshape(8, 4, 1, 128), axis=1)
        lower = lower.reshape(4, 2, 4, 1, 128)
        for j in range(4):
            cells = pl.ds(128 * j, 128)
            left, right = upper[j, 0], upper[j, 1]
            heavy[0, t, :, :, cells] = jnp.where(low_half3, left, pltpu.roll(right, 64, 2))
            heavy[1, t, :, :, cells] = jnp.where(low_half3, pltpu.roll(left, 64, 2), right)
            left, right = lower[j, 0], lower[j, 1]
            heavy[2, t, :, :, cells] = jnp.where(low_half3, left, pltpu.roll(right, 64, 2))
    column = lax.broadcasted_iota(jnp.int32, (16, 128), 0)
    sum_u = jnp.zeros((16, 128), F32)
    sum_a = jnp.zeros((16, 128), F32)
    for s in range(8):
        for other in range(2):
            hit = column == 5 * s // 4 + other
            sum_u = sum_u + jnp.where(hit, pltpu.roll(total[s], 64 - 16 * other, 1), 0.0)
            sum_a = sum_a + jnp.where(hit, pltpu.roll(total[s], 32 - 16 * other, 1), 0.0)
    lane = lax.broadcasted_iota(jnp.int32, (16, 128), 1)
    valid = (lane < ROWS) & (column < COLS)
    area = jnp.where(valid, sum_u[:, ROWS : ROWS + 1], 1.0)
    speed = sum_u / area
    reverse = sum_a / area
    coeff = jnp.where(valid, -thrust[...] * speed * (1.5 * speed + reverse), 0.0)
    cell = lax.broadcasted_iota(jnp.int32, (16, NY), 1)
    band = lax.broadcasted_iota(jnp.int32, (16, NY), 0)
    spread = jnp.where(cell * COLS // NY == band, 1.0, 0.0).astype(F32)
    exact = lax.Precision.HIGHEST
    per_column = lax.dot_general(
        row_basis[...], coeff, (((1,), (1,)), ((), ())), precision=exact, preferred_element_type=F32
    )
    forced[...] = jnp.dot(per_column, spread, precision=exact, preferred_element_type=F32)

    def transform(half, _):
        for group in range(2):
            for t in range(4):
                place(2 * half + group, t, 0)
        multiply(((0, 2 * half), (0, 2 * half + 1)))
        return 0

    lax.fori_loop(0, 2, transform, 0)
    fetch_inverses.wait()

    scale_x = [wave_x[c] for c in range(2)]
    scale_y = wave_y[0:1, :]

    def forward(block, carry):
        entries = []
        for i in range(4):
            z = 4 * block + i
            up = spectrum[2, jnp.minimum(z + 1, NZ - 1)]
            up = jnp.where(z + 1 < NZ, up, 0.0)
            down = spectrum[2, jnp.maximum(z - 1, 0)]
            down = jnp.where(z > 0, down, 0.0)
            entries.append(
                signed_x(spectrum[0, z], scale_x)
                + signed_y(spectrum[1, z], scale_y)
                + 0.5 * (up - down)
            )
        entries[0] = entries[0] - carry
        last = None
        for i in range(4):
            halves = []
            for q in range(2):
                cells = slice(256 * q, 256 * q + 256)
                total = inverses[block, 4 * i] * entries[0][:, cells]
                for j in range(1, 4):
                    total = total + inverses[block, 4 * i + j] * entries[j][:, cells]
                halves.append(total)
            last = jnp.concatenate(halves, axis=1)
            solved[4 * block + i] = last
        return last

    lax.fori_loop(0, BLOCKS, forward, jnp.zeros((16, NY), F32))

    def corrected(block, i, running):
        column = inverses[block, 4 * i + 3]
        return solved[4 * block + i] - jnp.concatenate([column, column], axis=1) * running

    def write(group):
        return pltpu.make_async_copy(
            staged.at[group], out.at[:, :, pl.ds(pl.multiple_of(8 * group, 8), 8), :], sems.at[group]
        )

    def backward(step, upper):
        group = 5 - step
        first = 2 * group
        running = upper
        pressure = [None] * 8
        for half in (1, 0):
            for i in range(4):
                pressure[4 * half + i] = corrected(first + half, i, running)
            running = pressure[4 * half]
        before = corrected(jnp.maximum(first - 1, 0), 3, running)
        before = jnp.where(group > 0, before, 0.0)
        pressure = [before] + pressure + [upper]
        for component in range(3):
            rows = []
            for z in range(8):
                here = pressure[z + 1]
                if component == 0:
                    slope = signed_x(here, scale_x)
                elif component == 1:
                    slope = signed_y(here, scale_y)
                else:
                    slope = 0.5 * (pressure[z + 2] - pressure[z])
                rows.append(spectrum[component, 8 * group + z] - slope)
            for r in range(16):
                sine, slot, inner = (r // 4) % 2, (r // 2) % 2, r % 2
                if r < 8:
                    mode = 4 * (2 * inner + (slot ^ parity[0])) + sine
                else:
                    mode = 4 * (r % 4) + 2 + sine
                staged[group, component, mode] = jnp.concatenate(
                    [rows[z][r : r + 1] for z in range(8)], axis=0
                )
        write(group).start()
        return running

    lax.fori_loop(0, 6, backward, jnp.zeros((16, NY), F32))
    for group in range(6):
        write(group).wait()


def across(parity, received, thrust, row_basis, wave_x, wave_y, inverses):
    tables = across_tables()
    smem = pl.BlockSpec(memory_space=pltpu.SMEM)
    vmem = pl.BlockSpec(memory_space=pltpu.VMEM)
    hbm = pl.BlockSpec(memory_space=pltpu.HBM)
    return pl.pallas_call(
        across_kernel,
        out_shape=jax.ShapeDtypeStruct((3, 16, NZ, NY), F32),
        in_specs=[smem] + [vmem] * 4 + [hbm] * 3,
        out_specs=hbm,
        scratch_shapes=[
            pltpu.VMEM((DESTS // 4, GROUP, 128), F32),
            pltpu.VMEM((BLOCKS, 16, 16, 256), F32),
            pltpu.VMEM((2, NY, NY), BF16),
            pltpu.VMEM((3, NZ, 16, NY), F32),
            pltpu.VMEM((NZ, 16, NY), F32),
            pltpu.VMEM((384, NY), BF16),
            pltpu.VMEM((384, NY), BF16),
            pltpu.VMEM((16, NY), F32),
            pltpu.VMEM((3, 4, 4, 1, NY), F32),
            pltpu.VMEM((6, 3, 16, 8, NY), F32),
            pltpu.SemaphoreType.DMA((12,)),
        ],
        compiler_params=pltpu.CompilerParams(vmem_limit_bytes=VMEM_BYTES),
        name="across",
    )(parity, thrust, row_basis, wave_x, wave_y, received, inverses, jnp.asarray(tables))


def body(adjoint, saved_grad, saved_u, disk_owner, disk_weight, row_x, thrust, block_inverse):
    axes = ("span", "stream")
    span = lax.axis_index("span")
    first_column = (5 * span // 4).astype(jnp.int32).reshape(1)
    sent = along(adjoint, saved_grad, saved_u, disk_owner, disk_weight, row_x, first_column)
    received = lax.all_to_all(
        sent.reshape(DESTS, 1, ROWS_SENT * 128), axes, split_axis=0, concat_axis=0, tiled=True
    ).reshape(DESTS // 4, GROUP, 128)

    device = lax.axis_index(axes).astype(jnp.int32)
    parity = device % 2
    row = jnp.arange(16, dtype=jnp.int32)
    sine, slot, inner = (row // 4) % 2, (row // 2) % 2, row % 2
    local = jnp.where(row < 8, 4 * inner + 2 * (slot ^ parity), 2 * (row % 4) + 1)
    mode = 8 * device + local
    wave = 2.0 * math.pi * mode.astype(F32) / NX
    wave_x = jnp.where(sine == 0, wave, -wave).reshape(2, 8, 1)
    wave_y = (2.0 * math.pi * jnp.arange(NY // 2, dtype=F32) / NY).reshape(1, 256)
    angle = (mode[:, None] * row_x[None, :] % NX).astype(F32) * (2.0 * math.pi / NX)
    basis = jnp.where(sine[:, None] == 0, jnp.cos(angle), jnp.sin(angle)) / math.sqrt(NX)
    row_basis = jnp.pad(basis, ((0, 0), (0, 128 - ROWS)))
    thrust_t = jnp.pad(thrust.T, ((0, 16 - COLS), (0, 128 - ROWS)))
    folded = block_inverse.reshape(2, 2, 2, BLOCKS, 16, 256)
    even = folded[:, :, 0].transpose(2, 3, 1, 0, 4)
    even = jnp.where(parity == 0, even, even[:, :, ::-1]).reshape(BLOCKS, 16, 1, 4, 256)
    odd = folded[:, :, 1].transpose(2, 3, 0, 1, 4).reshape(BLOCKS, 16, 1, 4, 256)
    inverses = jnp.concatenate([even, even, odd, odd], axis=2).reshape(BLOCKS, 16, 16, 256)
    return across(
        parity.reshape(1), received, thrust_t, row_basis, wave_x, wave_y, inverses
    )


def solution(mesh):
    in_specs = (
        P(None, "stream", "span", None),
        P(None, "stream", "span", None),
        P("stream", "span", None),
        P("stream", "span"),
        P("stream", "span"),
        P(),
        P(),
        P(("span", "stream"), None, None, None, None),
    )
    out_specs = P(None, ("span", "stream"), None, None)
    return jax.shard_map(body, mesh=mesh, in_specs=in_specs, out_specs=out_specs, check_vma=False)
```

```python
import functools
import math

import jax
import jax.numpy as jnp
import ml_dtypes
import numpy as np
from jax import lax
from jax.experimental import pallas as pl
from jax.experimental.pallas import tpu as pltpu
from jax.sharding import PartitionSpec as P

NX = 2048
NY = 512
NZ = 48
ROWS = 10
COLS = 10
HALF = NX // 2
BLOCKS = NZ // 4
DESTS = 128
ROWS_SENT = 74
GROUP = 4 * ROWS_SENT
F32 = jnp.float32
BF16 = jnp.bfloat16
VMEM_BYTES = 58 * 1024 * 1024


def split_table(values):
    high = values.astype(ml_dtypes.bfloat16)
    low = (values - high.astype(np.float64)).astype(ml_dtypes.bfloat16)
    return high, low


def wave_rows(mode, sine, length):
    phase = mode[:, None] * np.arange(length)[None, :] % NX
    angle = phase * (2.0 * np.pi / NX)
    return np.where(sine[:, None] == 0, np.cos(angle), np.sin(angle)) / np.sqrt(NX)


@functools.lru_cache(maxsize=None)
def along_tables():
    row = np.arange(HALF)
    sine, rest = (row // 4) % 2, row % 4
    odd = wave_rows(8 * (row // 8) + 2 * rest + 1, sine, HALF)
    row = np.arange(HALF // 2)
    sine, slot, inner = (row // 4) % 2, (row // 2) % 2, row % 2
    even = [
        wave_rows(8 * (2 * (row // 8) + (slot ^ kind)) + 4 * inner + 2 * kind, sine, HALF // 2)
        for kind in range(2)
    ]
    odd = np.stack(split_table(odd)).transpose(0, 2, 1).reshape(2, HALF, 2, HALF // 2)
    even = np.stack(split_table(np.stack(even))).transpose(1, 0, 3, 2)
    even = even.reshape(2, 2, HALF // 2, 2, HALF // 4)
    return odd.transpose(2, 0, 1, 3), even.transpose(3, 0, 1, 2, 4)


@functools.lru_cache(maxsize=None)
def across_tables():
    basis = np.arange(NY)
    phase = np.arange(NY)[:, None] * (basis % (NY // 2))[None, :] % NY
    angle = phase * (2.0 * np.pi / NY)
    values = np.where((basis // (NY // 2))[None, :] == 0, np.cos(angle), np.sin(angle))
    return np.stack(split_table(values / np.sqrt(NY)))


def split(value):
    high = value.astype(BF16)
    return high, (value - high.astype(F32)).astype(BF16)


def dot_nt(left, right):
    return lax.dot_general(left, right, (((1,), (1,)), ((), ())), preferred_element_type=F32)


def dot_nn(left, right):
    return jnp.dot(left, right, preferred_element_type=F32)


def couple(level, step, adjoint, grad, source_high, source_low):
    quarter = NX // 4
    rows = pl.ds(pl.multiple_of(16 * step, 16), 16)
    for start in range(0, quarter, 128):
        lanes = [pl.ds(quarter * n + start, 128) for n in range(4)]
        velocity = [[adjoint[j, level, rows, l].astype(F32) for l in lanes] for j in range(3)]
        for i in range(3):
            value = []
            for n, l in enumerate(lanes):
                total = velocity[0][n] * grad[3 * i, level, rows, l].astype(F32)
                for j in range(1, 3):
                    total = total + velocity[j][n] * grad[3 * i + j, level, rows, l].astype(F32)
                value.append(total)
            first, second = value[0] + value[2], value[1] + value[3]
            folded = (value[0] - value[2], value[1] - value[3], first + second, first - second)
            target = pl.ds(pl.multiple_of(64 * (3 * level + i) + 16 * step, 16), 16)
            for n in range(4):
                high, low = split(folded[n])
                source_high[target, lanes[n]] = high
                source_low[target, lanes[n]] = low


def along_kernel(
    row_x, first_column, owner, weight, adjoint_hbm, grad_hbm, saved_u_hbm, odd_hbm, even_hbm,
    out, adjoint, grad, saved_u, odd, even, source_high, source_low, onehot, extra, outbox, sems,
):
    copies = []
    for level in range(3):
        copies.append(pltpu.make_async_copy(adjoint_hbm.at[:, level], adjoint.at[:, level], sems.at[2 * level]))
        copies.append(pltpu.make_async_copy(grad_hbm.at[:, level], grad.at[:, level], sems.at[2 * level + 1]))
    fetch_u = pltpu.make_async_copy(saved_u_hbm, saved_u, sems.at[6])

    def fetch_tables(step):
        return (
            pltpu.make_async_copy(odd_hbm.at[step], odd.at[step], sems.at[7 + 2 * step]),
            pltpu.make_async_copy(even_hbm.at[step], even.at[step], sems.at[8 + 2 * step]),
        )

    early, late = fetch_tables(0), fetch_tables(1)
    for copy in copies[:4]:
        copy.start()

    lane = lax.broadcasted_iota(jnp.int32, (1, 128), 1) % 16
    wanted = jnp.full((1, 128), -1, jnp.int32)
    for r in range(ROWS):
        wanted = jnp.where(lane == r, row_x[r], wanted)

    def mark(step, _):
        rows = pl.ds(pl.multiple_of(256 * step, 256), 256)
        cell = lax.broadcasted_iota(jnp.int32, (256, 128), 0) + 256 * step
        onehot[rows, :] = jnp.where(cell == wanted, 1.0, 0.0).astype(BF16)
        return 0

    lax.fori_loop(0, NX // 256, mark, 0)

    def couple_rows(level):
        def rows_of(step, _):
            couple(level, step, adjoint, grad, source_high, source_low)
            return 0

        lax.fori_loop(0, 4, rows_of, 0)

    sums_u, sums_a, masked = [], [], []

    def disk_level(level):
        column_u = dot_nn(saved_u[level], onehot[...])
        column_a = dot_nn(adjoint[0, level], onehot[...]).astype(BF16)
        column_u = jnp.where(lane == ROWS, 1.0, column_u).astype(BF16)
        own = owner[level : level + 1, :]
        heavy = weight[level : level + 1, :]
        masked.append(jnp.where(own >= 0, heavy, 0.0))
        row = lax.broadcasted_iota(jnp.int32, (8, 64), 0)
        rest = jnp.where(own == first_column[0] + row % 2, heavy, 0.0)
        for _ in range(3):
            part = rest.astype(BF16)
            rest = rest - part.astype(F32)
            sums_u.append(dot_nn(part, column_u))
            sums_a.append(dot_nn(part, column_a))

    def disk_rows():
        sum_u = functools.reduce(jnp.add, sums_u)
        sum_a = functools.reduce(jnp.add, sums_a)
        place = lax.broadcasted_iota(jnp.int32, (1, 128), 1) // 16
        sums = jnp.where(place == 4, sum_u[0:1], sum_u[1:2])
        sums = jnp.where(place == 6, sum_a[0:1], jnp.where(place == 7, sum_a[1:2], sums))
        last = jnp.concatenate([masked[2], jnp.zeros((1, 64), F32)], axis=1)
        last = jnp.where(place < 4, last, sums)
        return jnp.concatenate([jnp.concatenate(masked[:2], axis=1), last], axis=0)

    first_slot = lax.broadcasted_iota(jnp.int32, (8, 128), 0) % 4 < 2
    low_half = lax.broadcasted_iota(jnp.int32, (8, 128), 1) < 64

    def product(rows, span, high, low):
        cells = pl.ds(span, high.shape[0])
        result = dot_nn(source_high[rows, cells], high)
        result = result + dot_nn(source_low[rows, cells], high)
        return result + dot_nn(source_high[rows, cells], low)

    def send(step):
        part = pl.ds(16 * step, 16)
        return pltpu.make_async_copy(outbox.at[part], out.at[part], sems.at[11 + step])

    def fill(step, start, count, tiles):
        rows = pl.ds(start, count)

        def turned(value, tile, block):
            lanes = slice(128 * block, 128 * block + 128)
            begin = 128 * tile - start
            if tile < 4:
                part = value[begin : begin + 128, lanes]
            else:
                part = jnp.concatenate([value[begin : begin + 64, lanes]] * 2, axis=0)
            return part.T

        def store(dest, tile, value):
            place = ROWS_SENT * (dest % 4) + 8 * tile
            outbox[16 * step + dest // 4, pl.ds(place, 8), :] = value

        kinds = [
            product(rows, HALF + HALF // 2 * k, even[step, k, 0], even[step, k, 1]) for k in range(2)
        ]
        rest = product(rows, 0, odd[step, 0], odd[step, 1])
        for tile in tiles:
            for block in range(2):
                pair = [turned(value, tile, block) for value in kinds]
                for side in range(2):
                    single = turned(rest, tile, 2 * block + side)
                    for index in range(16):
                        dest = 32 * block + 16 * side + index
                        part = slice(8 * (dest // 2 % 16), 8 * (dest // 2 % 16) + 8)
                        even_part = jnp.where(first_slot, pair[dest % 2][part], pair[1 - dest % 2][part])
                        odd_part = single[8 * index : 8 * index + 8]
                        if tile < 4:
                            store(dest, tile, even_part)
                            store(dest, 4 + tile, odd_part)
                        else:
                            store(dest, 8, jnp.where(low_half, even_part, odd_part))

    def wait_for(level):
        copies[2 * level].wait()
        copies[2 * level + 1].wait()

    wait_for(0)
    for copy in early:
        copy.start()
    couple_rows(0)
    wait_for(1)
    fetch_u.start()
    for copy in copies[4:]:
        copy.start()
    couple_rows(1)
    for copy in early:
        copy.wait()
    for copy in late:
        copy.start()
    fetch_u.wait()
    fill(0, 0, 384, range(3))
    disk_level(0)
    disk_level(1)
    wait_for(2)
    for copy in late:
        copy.wait()
    for step in range(4):
        couple(2, step, adjoint, grad, source_high, source_low)
    disk_level(2)
    extra[...] = disk_rows()
    fill(1, 0, 384, range(3))

    def finish(step, _):
        for dest in range(64):
            outbox[16 * step + dest // 4, pl.ds(ROWS_SENT * (dest % 4) + 72, 2), :] = extra[...]
        fill(step, 384, 192, range(3, 5))
        send(step).start()
        return 0

    lax.fori_loop(0, 2, finish, 0)
    send(0).wait()
    send(1).wait()


def along(adjoint, grad, saved_u, owner, weight, row_x, first_column):
    odd, even = along_tables()
    smem = pl.BlockSpec(memory_space=pltpu.SMEM)
    vmem = pl.BlockSpec(memory_space=pltpu.VMEM)
    hbm = pl.BlockSpec(memory_space=pltpu.HBM)
    return pl.pallas_call(
        along_kernel,
        out_shape=jax.ShapeDtypeStruct((DESTS // 4, GROUP, 128), F32),
        in_specs=[smem, smem, vmem, vmem, hbm, hbm, hbm, hbm, hbm],
        out_specs=hbm,
        scratch_shapes=[
            pltpu.VMEM((3, 3, 64, NX), BF16),
            pltpu.VMEM((9, 3, 64, NX), BF16),
            pltpu.VMEM((3, 64, NX), BF16),
            pltpu.VMEM(odd.shape, BF16),
            pltpu.VMEM(even.shape, BF16),
            pltpu.VMEM((576, NX), BF16),
            pltpu.VMEM((576, NX), BF16),
            pltpu.VMEM((NX, 128), BF16),
            pltpu.VMEM((2, 128), F32),
            pltpu.VMEM((DESTS // 4, GROUP, 128), F32),
            pltpu.SemaphoreType.DMA((13,)),
        ],
        compiler_params=pltpu.CompilerParams(vmem_limit_bytes=VMEM_BYTES),
        name="along",
    )(row_x, first_column, owner, weight, adjoint, grad, saved_u, jnp.asarray(odd), jnp.asarray(even))


def signed_x(value, scale):
    return jnp.concatenate(
        [scale[c] * pltpu.roll(value[8 * c : 8 * c + 8], 4, 0) for c in range(2)], axis=0
    )


def signed_y(value, scale):
    return jnp.concatenate([scale * value[:, 256:], -scale * value[:, :256]], axis=1)


def across_kernel(
    parity, thrust, row_basis, wave_x, wave_y, received_hbm, inverses_hbm, tables_hbm,
    out, received, extras, inverses, tables, spectrum, solved, high_0, high_1, low_0, low_1, forced, heavy, turned, staged, sems,
):
    fetch_extras = []
    for t in range(4):
        window = pl.ds((ROWS_SENT * t + 72) // 8 * 8, 8)
        fetch_extras.append(
            pltpu.make_async_copy(received_hbm.at[:, :, window], extras.at[t], sems.at[12 + t])
        )
    fetch = [
        pltpu.make_async_copy(received_hbm.at[:, group], received.at[:, group], sems.at[6 + group])
        for group in range(4)
    ]
    fetch_tables = pltpu.make_async_copy(tables_hbm, tables, sems.at[10])
    fetch_inverses = pltpu.make_async_copy(inverses_hbm, inverses, sems.at[11])
    for copy in fetch_extras + [fetch[0], fetch_tables]:
        copy.start()
    grids = ((high_0, low_0), (high_1, low_1))
    low_half = lax.broadcasted_iota(jnp.int32, (1, 128), 1) < 64
    low_half3 = low_half[None]

    def place(unit, parts):
        high_grid, low_grid = grids[unit % 2]
        for n, (component, group) in enumerate(parts):
            for t in range(4):
                for inner in range(3):
                    pair = 3 * inner + component
                    target = pl.ds(192 * n + 16 * (3 * t + inner), 16)
                    for j in range(4):
                        cells = pl.ds(128 * j, 128)
                        values = []
                        for kind in range(2):
                            tile, side = (4 * kind + pair // 2, pair % 2) if pair < 8 else (8, kind)
                            rows = pl.ds(ROWS_SENT * t + 8 * tile, 8)
                            left = received[2 * j, group, rows, :]
                            right = received[2 * j + 1, group, rows, :]
                            if side == 0:
                                value = jnp.where(low_half, left, pltpu.roll(right, 64, 1))
                            else:
                                value = jnp.where(low_half, pltpu.roll(left, 64, 1), right)
                            if component == 0:
                                disk = heavy[inner, t, group, :, cells]
                                value = value + disk * forced[pl.ds(8 * kind, 8), cells]
                            values.append(value)
                        high, low = split(jnp.concatenate(values, axis=0))
                        high_grid[target, cells] = high
                        low_grid[target, cells] = low

    def multiply(unit, parts):
        high_grid, low_grid = grids[unit % 2]
        result = dot_nn(high_grid[...], tables[0])
        result = result + dot_nn(low_grid[...], tables[0])
        result = result + dot_nn(high_grid[...], tables[1])
        for n, (component, group) in enumerate(parts):
            spectrum[component, pl.ds(12 * group, 12)] = result[192 * n : 192 * n + 192].reshape(12, 16, NY)

    for copy in fetch_extras:
        copy.wait()
    for copy in [fetch[1], fetch_inverses] + fetch[2:]:
        copy.start()
    total = jnp.zeros((8, 1, 128), F32)
    for t in range(4):
        start = (ROWS_SENT * t + 72) % 8
        upper = extras[t, :, :, pl.ds(start, 1), :].reshape(4, 2, 4, 1, 128)
        lower = extras[t, :, :, pl.ds(start + 1, 1), :]
        total = total + jnp.sum(lower, axis=1)
        lower = lower.reshape(4, 2, 4, 1, 128)
        for j in range(4):
            cells = pl.ds(128 * j, 128)
            left, right = upper[j, 0], upper[j, 1]
            heavy[0, t, :, :, cells] = jnp.where(low_half3, left, pltpu.roll(right, 64, 2))
            heavy[1, t, :, :, cells] = jnp.where(low_half3, pltpu.roll(left, 64, 2), right)
            left, right = lower[j, 0], lower[j, 1]
            heavy[2, t, :, :, cells] = jnp.where(low_half3, left, pltpu.roll(right, 64, 2))
    column = lax.broadcasted_iota(jnp.int32, (16, 128), 0)
    sum_u = jnp.zeros((16, 128), F32)
    sum_a = jnp.zeros((16, 128), F32)
    for s in range(8):
        for other in range(2):
            hit = column == 5 * s // 4 + other
            sum_u = sum_u + jnp.where(hit, pltpu.roll(total[s], 64 - 16 * other, 1), 0.0)
            sum_a = sum_a + jnp.where(hit, pltpu.roll(total[s], 32 - 16 * other, 1), 0.0)
    lane = lax.broadcasted_iota(jnp.int32, (16, 128), 1)
    valid = (lane < ROWS) & (column < COLS)
    area = jnp.where(valid, sum_u[:, ROWS : ROWS + 1], 1.0)
    speed = sum_u / area
    reverse = sum_a / area
    coeff = jnp.where(valid, -thrust[...] * speed * (1.5 * speed + reverse), 0.0)
    cell = lax.broadcasted_iota(jnp.int32, (16, NY), 1)
    band = lax.broadcasted_iota(jnp.int32, (16, NY), 0)
    spread = jnp.where(cell * COLS // NY == band, 1.0, 0.0).astype(F32)
    exact = lax.Precision.HIGHEST
    per_column = lax.dot_general(
        row_basis[...], coeff, (((1,), (1,)), ((), ())), precision=exact, preferred_element_type=F32
    )
    forced[...] = jnp.dot(per_column, spread, precision=exact, preferred_element_type=F32)

    scale_x = [wave_x[c] for c in range(2)]
    scale_y = wave_y[0:1, :]

    def forward(block, carry):
        entries = []
        for i in range(4):
            z = 4 * block + i
            up = spectrum[2, z + 1] if z + 1 < NZ else 0.0
            down = spectrum[2, z - 1] if z > 0 else 0.0
            entries.append(
                signed_x(spectrum[0, z], scale_x)
                + signed_y(spectrum[1, z], scale_y)
                + 0.5 * (up - down)
            )
        entries[0] = entries[0] - carry
        last = None
        for i in range(4):
            halves = []
            for q in range(2):
                cells = slice(256 * q, 256 * q + 256)
                total = inverses[block, 4 * i] * entries[0][:, cells]
                for j in range(1, 4):
                    total = total + inverses[block, 4 * i + j] * entries[j][:, cells]
                halves.append(total)
            last = jnp.concatenate(halves, axis=1)
            solved[4 * block + i] = last
        return last

    parts = [[(component, group) for component in range(3)] for group in range(4)]
    carry = jnp.zeros((16, NY), F32)
    fetch[0].wait()
    place(0, parts[0])
    fetch_tables.wait()
    for group in range(4):
        if group < 3:
            fetch[group + 1].wait()
        if group == 1:
            fetch_inverses.wait()
        multiply(group, parts[group])
        if group < 3:
            place(group + 1, parts[group + 1])
        if group > 0:
            for block in range(max(3 * group - 4, 0), 3 * group - 1):
                carry = forward(block, carry)
    for block in range(8, BLOCKS):
        carry = forward(block, carry)

    def corrected(block, i, running):
        column = inverses[block, 4 * i + 3]
        return solved[4 * block + i] - jnp.concatenate([column, column], axis=1) * running

    def write(group):
        return pltpu.make_async_copy(
            staged.at[group], out.at[:, :, pl.ds(pl.multiple_of(8 * group, 8), 8), :], sems.at[group]
        )

    def backward(step, upper):
        group = 5 - step
        first = 2 * group
        running = upper
        pressure = [None] * 8
        for half in (1, 0):
            for i in range(4):
                pressure[4 * half + i] = corrected(first + half, i, running)
            running = pressure[4 * half]
        before = corrected(jnp.maximum(first - 1, 0), 3, running)
        before = jnp.where(group > 0, before, 0.0)
        pressure = [before] + pressure + [upper]
        for component in range(3):
            for z in range(8):
                here = pressure[z + 1]
                if component == 0:
                    slope = signed_x(here, scale_x)
                elif component == 1:
                    slope = signed_y(here, scale_y)
                else:
                    slope = 0.5 * (pressure[z + 2] - pressure[z])
                value = spectrum[component, 8 * group + z] - slope
                for j in range(4):
                    turned[component, j, pl.ds(16 * z, 16), :] = value[:, 128 * j : 128 * j + 128]
            for r in range(16):
                sine, slot, inner = (r // 4) % 2, (r // 2) % 2, r % 2
                if r < 8:
                    mode = 4 * (2 * inner + (slot ^ parity[0])) + sine
                else:
                    mode = 4 * (r % 4) + 2 + sine
                for j in range(4):
                    cells = pl.ds(128 * j, 128)
                    staged[group, component, mode, :, cells] = turned[component, j, pl.ds(r, 8, stride=16), :]
        write(group).start()
        return running

    lax.fori_loop(0, 6, backward, jnp.zeros((16, NY), F32))
    for group in range(6):
        write(group).wait()


def across(parity, received, thrust, row_basis, wave_x, wave_y, inverses):
    tables = across_tables()
    smem = pl.BlockSpec(memory_space=pltpu.SMEM)
    vmem = pl.BlockSpec(memory_space=pltpu.VMEM)
    hbm = pl.BlockSpec(memory_space=pltpu.HBM)
    return pl.pallas_call(
        across_kernel,
        out_shape=jax.ShapeDtypeStruct((3, 16, NZ, NY), F32),
        in_specs=[smem] + [vmem] * 4 + [hbm] * 3,
        out_specs=hbm,
        scratch_shapes=[
            pltpu.VMEM((8, 4, GROUP, 128), F32),
            pltpu.VMEM((4, 8, 4, 8, 128), F32),
            pltpu.VMEM((BLOCKS, 16, 16, 256), F32),
            pltpu.VMEM((2, NY, NY), BF16),
            pltpu.VMEM((3, NZ, 16, NY), F32),
            pltpu.VMEM((NZ, 16, NY), F32),
            pltpu.VMEM((576, NY), BF16),
            pltpu.VMEM((576, NY), BF16),
            pltpu.VMEM((576, NY), BF16),
            pltpu.VMEM((576, NY), BF16),
            pltpu.VMEM((16, NY), F32),
            pltpu.VMEM((3, 4, 4, 1, NY), F32),
            pltpu.VMEM((3, 4, 128, 128), F32),
            pltpu.VMEM((6, 3, 16, 8, NY), F32),
            pltpu.SemaphoreType.DMA((16,)),
        ],
        compiler_params=pltpu.CompilerParams(vmem_limit_bytes=VMEM_BYTES),
        name="across",
    )(parity, thrust, row_basis, wave_x, wave_y, received, inverses, jnp.asarray(tables))


def body(adjoint, saved_grad, saved_u, disk_owner, disk_weight, row_x, thrust, block_inverse):
    axes = ("span", "stream")
    span = lax.axis_index("span")
    first_column = (5 * span // 4).astype(jnp.int32).reshape(1)
    sent = along(adjoint, saved_grad, saved_u, disk_owner, disk_weight, row_x, first_column)
    received = lax.all_to_all(
        sent.reshape(DESTS, 1, ROWS_SENT * 128), axes, split_axis=0, concat_axis=0, tiled=True
    ).reshape(8, 4, GROUP, 128)

    device = lax.axis_index(axes).astype(jnp.int32)
    parity = device % 2
    row = jnp.arange(16, dtype=jnp.int32)
    sine, slot, inner = (row // 4) % 2, (row // 2) % 2, row % 2
    local = jnp.where(row < 8, 4 * inner + 2 * (slot ^ parity), 2 * (row % 4) + 1)
    mode = 8 * device + local
    wave = 2.0 * math.pi * mode.astype(F32) / NX
    wave_x = jnp.where(sine == 0, wave, -wave).reshape(2, 8, 1)
    wave_y = (2.0 * math.pi * jnp.arange(NY // 2, dtype=F32) / NY).reshape(1, 256)
    angle = (mode[:, None] * row_x[None, :] % NX).astype(F32) * (2.0 * math.pi / NX)
    basis = jnp.where(sine[:, None] == 0, jnp.cos(angle), jnp.sin(angle)) / math.sqrt(NX)
    row_basis = jnp.pad(basis, ((0, 0), (0, 128 - ROWS)))
    thrust_t = jnp.pad(thrust.T, ((0, 16 - COLS), (0, 128 - ROWS)))
    folded = block_inverse.reshape(2, 2, 2, BLOCKS, 16, 256)
    even = folded[:, :, 0].transpose(2, 3, 1, 0, 4)
    even = jnp.where(parity == 0, even, even[:, :, ::-1]).reshape(BLOCKS, 16, 1, 4, 256)
    odd = folded[:, :, 1].transpose(2, 3, 0, 1, 4).reshape(BLOCKS, 16, 1, 4, 256)
    inverses = jnp.concatenate([even, even, odd, odd], axis=2).reshape(BLOCKS, 16, 16, 256)
    return across(
        parity.reshape(1), received, thrust_t, row_basis, wave_x, wave_y, inverses
    )


def solution(mesh):
    in_specs = (
        P(None, "stream", "span", None),
        P(None, "stream", "span", None),
        P("stream", "span", None),
        P("stream", "span"),
        P("stream", "span"),
        P(),
        P(),
        P(("span", "stream"), None, None, None, None),
    )
    out_specs = P(None, ("span", "stream"), None, None)
    return jax.shard_map(body, mesh=mesh, in_specs=in_specs, out_specs=out_specs, check_vma=False)
```

```python
import functools
import math

import jax
import jax.numpy as jnp
import ml_dtypes
import numpy as np
from jax import lax
from jax.experimental import pallas as pl
from jax.experimental.pallas import tpu as pltpu
from jax.sharding import PartitionSpec as P

NX = 2048
NY = 512
NZ = 48
ROWS = 10
COLS = 10
HALF = NX // 2
BLOCKS = NZ // 4
DESTS = 128
ROWS_SENT = 74
GROUP = 4 * ROWS_SENT
F32 = jnp.float32
BF16 = jnp.bfloat16
VMEM_BYTES = 58 * 1024 * 1024


def split_table(values):
    high = values.astype(ml_dtypes.bfloat16)
    low = (values - high.astype(np.float64)).astype(ml_dtypes.bfloat16)
    return high, low


def wave_rows(mode, sine, length):
    phase = mode[:, None] * np.arange(length)[None, :] % NX
    angle = phase * (2.0 * np.pi / NX)
    return np.where(sine[:, None] == 0, np.cos(angle), np.sin(angle)) / np.sqrt(NX)


@functools.lru_cache(maxsize=None)
def along_tables():
    row = np.arange(HALF)
    sine, rest = (row // 4) % 2, row % 4
    odd = wave_rows(8 * (row // 8) + 2 * rest + 1, sine, HALF)
    row = np.arange(HALF // 2)
    sine, slot, inner = (row // 4) % 2, (row // 2) % 2, row % 2
    even = [
        wave_rows(8 * (2 * (row // 8) + (slot ^ kind)) + 4 * inner + 2 * kind, sine, HALF // 2)
        for kind in range(2)
    ]
    odd = np.stack(split_table(odd)).transpose(0, 2, 1).reshape(2, HALF, 2, HALF // 2)
    even = np.stack(split_table(np.stack(even))).transpose(1, 0, 3, 2)
    even = even.reshape(2, 2, HALF // 2, 2, HALF // 4)
    return odd.transpose(2, 0, 1, 3), even.transpose(3, 0, 1, 2, 4)


@functools.lru_cache(maxsize=None)
def across_tables():
    basis = np.arange(NY)
    phase = np.arange(NY)[:, None] * (basis % (NY // 2))[None, :] % NY
    angle = phase * (2.0 * np.pi / NY)
    values = np.where((basis // (NY // 2))[None, :] == 0, np.cos(angle), np.sin(angle))
    return np.stack(split_table(values / np.sqrt(NY)))


def split(value):
    high = value.astype(BF16)
    return high, (value - high.astype(F32)).astype(BF16)


def dot_nt(left, right):
    return lax.dot_general(left, right, (((1,), (1,)), ((), ())), preferred_element_type=F32)


def dot_nn(left, right):
    return jnp.dot(left, right, preferred_element_type=F32)


def couple(level, step, adjoint, grad, source_high, source_low):
    quarter = NX // 4
    rows = pl.ds(pl.multiple_of(16 * step, 16), 16)
    for start in range(0, quarter, 128):
        lanes = [pl.ds(quarter * n + start, 128) for n in range(4)]
        velocity = [[adjoint[j, level, rows, l].astype(F32) for l in lanes] for j in range(3)]
        for i in range(3):
            value = []
            for n, l in enumerate(lanes):
                total = velocity[0][n] * grad[3 * i, level, rows, l].astype(F32)
                for j in range(1, 3):
                    total = total + velocity[j][n] * grad[3 * i + j, level, rows, l].astype(F32)
                value.append(total)
            first, second = value[0] + value[2], value[1] + value[3]
            folded = (value[0] - value[2], value[1] - value[3], first + second, first - second)
            target = pl.ds(pl.multiple_of(64 * (3 * level + i) + 16 * step, 16), 16)
            for n in range(4):
                high, low = split(folded[n])
                source_high[target, lanes[n]] = high
                source_low[target, lanes[n]] = low


def along_kernel(
    row_x, first_column, owner, weight, adjoint_hbm, grad_hbm, saved_u_hbm, odd_hbm, even_hbm,
    out, adjoint, grad, saved_u, odd, even, source_high, source_low, onehot, outbox, sems,
):
    copies = []
    for level in range(3):
        copies.append(pltpu.make_async_copy(adjoint_hbm.at[:, level], adjoint.at[:, level], sems.at[2 * level]))
        copies.append(pltpu.make_async_copy(grad_hbm.at[:, level], grad.at[:, level], sems.at[2 * level + 1]))
    fetch_u = pltpu.make_async_copy(saved_u_hbm, saved_u, sems.at[6])

    def fetch_tables(step):
        return (
            pltpu.make_async_copy(odd_hbm.at[step], odd.at[step], sems.at[7 + 2 * step]),
            pltpu.make_async_copy(even_hbm.at[step], even.at[step], sems.at[8 + 2 * step]),
        )

    early, late = fetch_tables(0), fetch_tables(1)
    for copy in copies + [fetch_u] + list(early) + list(late):
        copy.start()

    lane = lax.broadcasted_iota(jnp.int32, (1, 128), 1) % 16
    wanted = jnp.full((1, 128), -1, jnp.int32)
    for r in range(ROWS):
        wanted = jnp.where(lane == r, row_x[r], wanted)

    def mark(step, _):
        rows = pl.ds(pl.multiple_of(256 * step, 256), 256)
        cell = lax.broadcasted_iota(jnp.int32, (256, 128), 0) + 256 * step
        onehot[rows, :] = jnp.where(cell == wanted, 1.0, 0.0).astype(BF16)
        return 0

    lax.fori_loop(0, NX // 256, mark, 0)

    def couple_rows(level):
        def rows_of(step, _):
            couple(level, step, adjoint, grad, source_high, source_low)
            return 0

        lax.fori_loop(0, 4, rows_of, 0)

    sums_u, sums_a, masked = [], [], []

    def disk_level(level):
        column_u = dot_nn(saved_u[level], onehot[...])
        column_a = dot_nn(adjoint[0, level], onehot[...]).astype(BF16)
        column_u = jnp.where(lane == ROWS, 1.0, column_u).astype(BF16)
        own = owner[level : level + 1, :]
        heavy = weight[level : level + 1, :]
        masked.append(jnp.where(own >= 0, heavy, 0.0))
        row = lax.broadcasted_iota(jnp.int32, (8, 64), 0)
        rest = jnp.where(own == first_column[0] + row % 2, heavy, 0.0)
        for _ in range(3):
            part = rest.astype(BF16)
            rest = rest - part.astype(F32)
            sums_u.append(dot_nn(part, column_u))
            sums_a.append(dot_nn(part, column_a))

    def disk_rows():
        sum_u = functools.reduce(jnp.add, sums_u)
        sum_a = functools.reduce(jnp.add, sums_a)
        place = lax.broadcasted_iota(jnp.int32, (1, 128), 1) // 16
        sums = jnp.where(place == 4, sum_u[0:1], sum_u[1:2])
        sums = jnp.where(place == 6, sum_a[0:1], jnp.where(place == 7, sum_a[1:2], sums))
        last = jnp.concatenate([masked[2], jnp.zeros((1, 64), F32)], axis=1)
        last = jnp.where(place < 4, last, sums)
        return jnp.concatenate([jnp.concatenate(masked[:2], axis=1), last], axis=0)

    first_slot = lax.broadcasted_iota(jnp.int32, (8, 128), 0) % 4 < 2
    low_half = lax.broadcasted_iota(jnp.int32, (8, 128), 1) < 64

    def product(rows, span, high, low):
        cells = pl.ds(span, high.shape[0])
        result = dot_nn(source_high[rows, cells], high)
        result = result + dot_nn(source_low[rows, cells], high)
        return result + dot_nn(source_high[rows, cells], low)

    def send(step, block):
        part = pl.ds(16 * step + 8 * block, 8)
        return pltpu.make_async_copy(outbox.at[part], out.at[part], sems.at[11 + 2 * step + block])

    def fill(step, start, count, tiles, extra=None):
        rows = pl.ds(start, count)

        def turned(value, tile, block):
            lanes = slice(128 * block, 128 * block + 128)
            begin = 128 * tile - start
            if tile < 4:
                part = value[begin : begin + 128, lanes]
            else:
                part = jnp.concatenate([value[begin : begin + 64, lanes]] * 2, axis=0)
            return part.T

        def store(dest, tile, value):
            place = ROWS_SENT * (dest % 4) + 8 * tile
            outbox[16 * step + dest // 4, pl.ds(place, 8), :] = value

        kinds = [
            product(rows, HALF + HALF // 2 * k, even[step, k, 0], even[step, k, 1]) for k in range(2)
        ]
        for block in range(2):
            modes = pl.ds(256 * block, 256)
            rest = product(rows, 0, odd[step, 0, :, modes], odd[step, 1, :, modes])
            for tile in tiles:
                pair = [turned(value, tile, block) for value in kinds]
                for side in range(2):
                    single = turned(rest, tile, side)
                    for index in range(16):
                        dest = 32 * block + 16 * side + index
                        part = slice(8 * (dest // 2 % 16), 8 * (dest // 2 % 16) + 8)
                        even_part = jnp.where(first_slot, pair[dest % 2][part], pair[1 - dest % 2][part])
                        odd_part = single[8 * index : 8 * index + 8]
                        if tile < 4:
                            store(dest, tile, even_part)
                            store(dest, 4 + tile, odd_part)
                        else:
                            store(dest, 8, jnp.where(low_half, even_part, odd_part))
            if extra is not None:
                for dest in range(32 * block, 32 * block + 32):
                    outbox[16 * step + dest // 4, pl.ds(ROWS_SENT * (dest % 4) + 72, 2), :] = extra
                send(step, block).start()

    def wait_for(level):
        copies[2 * level].wait()
        copies[2 * level + 1].wait()

    wait_for(0)
    couple_rows(0)
    wait_for(1)
    couple_rows(1)
    fetch_u.wait()
    disk_level(0)
    disk_level(1)
    wait_for(2)
    for copy in early:
        copy.wait()
    for step in range(4):
        couple(2, step, adjoint, grad, source_high, source_low)
    disk_level(2)
    extra = disk_rows()
    fill(0, 0, 384, range(3))
    fill(0, 384, 192, range(3, 5), extra)
    for copy in late:
        copy.wait()
    fill(1, 0, 576, range(5), extra)
    for step in range(2):
        for block in range(2):
            send(step, block).wait()


def along(adjoint, grad, saved_u, owner, weight, row_x, first_column):
    odd, even = along_tables()
    smem = pl.BlockSpec(memory_space=pltpu.SMEM)
    vmem = pl.BlockSpec(memory_space=pltpu.VMEM)
    hbm = pl.BlockSpec(memory_space=pltpu.HBM)
    return pl.pallas_call(
        along_kernel,
        out_shape=jax.ShapeDtypeStruct((DESTS // 4, GROUP, 128), F32),
        in_specs=[smem, smem, vmem, vmem, hbm, hbm, hbm, hbm, hbm],
        out_specs=hbm,
        scratch_shapes=[
            pltpu.VMEM((3, 3, 64, NX), BF16),
            pltpu.VMEM((9, 3, 64, NX), BF16),
            pltpu.VMEM((3, 64, NX), BF16),
            pltpu.VMEM(odd.shape, BF16),
            pltpu.VMEM(even.shape, BF16),
            pltpu.VMEM((576, NX), BF16),
            pltpu.VMEM((576, NX), BF16),
            pltpu.VMEM((NX, 128), BF16),
            pltpu.VMEM((DESTS // 4, GROUP, 128), F32),
            pltpu.SemaphoreType.DMA((15,)),
        ],
        compiler_params=pltpu.CompilerParams(vmem_limit_bytes=VMEM_BYTES),
        name="along",
    )(row_x, first_column, owner, weight, adjoint, grad, saved_u, jnp.asarray(odd), jnp.asarray(even))


def signed_x(value, scale):
    return jnp.concatenate(
        [scale[c] * pltpu.roll(value[8 * c : 8 * c + 8], 4, 0) for c in range(2)], axis=0
    )


def signed_y(value, scale):
    return jnp.concatenate([scale * value[:, 256:], -scale * value[:, :256]], axis=1)


def across_kernel(
    parity, thrust, row_basis, wave_x, wave_y, received_hbm, inverses_hbm, tables_hbm,
    out, received, extras, inverses, tables, spectrum, solved, high_0, high_1, low_0, low_1, forced, heavy, turned, staged, sems,
):
    fetch_extras = []
    for t in range(4):
        window = pl.ds((ROWS_SENT * t + 72) // 8 * 8, 8)
        fetch_extras.append(
            pltpu.make_async_copy(received_hbm.at[:, :, window], extras.at[t], sems.at[12 + t])
        )
    fetch = [
        pltpu.make_async_copy(received_hbm.at[:, group], received.at[:, group], sems.at[6 + group])
        for group in range(4)
    ]
    fetch_tables = pltpu.make_async_copy(tables_hbm, tables, sems.at[10])
    fetch_inverses = pltpu.make_async_copy(inverses_hbm, inverses, sems.at[11])
    for copy in fetch_extras + [fetch[0], fetch_tables, fetch[1], fetch_inverses] + fetch[2:]:
        copy.start()
    grids = ((high_0, low_0), (high_1, low_1))
    low_half = lax.broadcasted_iota(jnp.int32, (1, 128), 1) < 64
    low_half3 = low_half[None]

    def place(unit, parts):
        high_grid, low_grid = grids[unit % 2]
        for n, (component, group) in enumerate(parts):
            for t in range(4):
                for inner in range(3):
                    pair = 3 * inner + component
                    target = pl.ds(192 * n + 16 * (3 * t + inner), 16)
                    for j in range(4):
                        cells = pl.ds(128 * j, 128)
                        values = []
                        for kind in range(2):
                            tile, side = (4 * kind + pair // 2, pair % 2) if pair < 8 else (8, kind)
                            rows = pl.ds(ROWS_SENT * t + 8 * tile, 8)
                            left = received[2 * j, group, rows, :]
                            right = received[2 * j + 1, group, rows, :]
                            if side == 0:
                                value = jnp.where(low_half, left, pltpu.roll(right, 64, 1))
                            else:
                                value = jnp.where(low_half, pltpu.roll(left, 64, 1), right)
                            if component == 0:
                                disk = heavy[inner, t, group, :, cells]
                                value = value + disk * forced[pl.ds(8 * kind, 8), cells]
                            values.append(value)
                        high, low = split(jnp.concatenate(values, axis=0))
                        high_grid[target, cells] = high
                        low_grid[target, cells] = low

    def multiply(unit, parts):
        high_grid, low_grid = grids[unit % 2]
        result = dot_nn(high_grid[...], tables[0])
        result = result + dot_nn(low_grid[...], tables[0])
        result = result + dot_nn(high_grid[...], tables[1])
        for n, (component, group) in enumerate(parts):
            spectrum[component, pl.ds(12 * group, 12)] = result[192 * n : 192 * n + 192].reshape(12, 16, NY)

    for copy in fetch_extras:
        copy.wait()
    total = jnp.zeros((8, 1, 128), F32)
    for t in range(4):
        start = (ROWS_SENT * t + 72) % 8
        upper = extras[t, :, :, pl.ds(start, 1), :].reshape(4, 2, 4, 1, 128)
        lower = extras[t, :, :, pl.ds(start + 1, 1), :]
        total = total + jnp.sum(lower, axis=1)
        lower = lower.reshape(4, 2, 4, 1, 128)
        for j in range(4):
            cells = pl.ds(128 * j, 128)
            left, right = upper[j, 0], upper[j, 1]
            heavy[0, t, :, :, cells] = jnp.where(low_half3, left, pltpu.roll(right, 64, 2))
            heavy[1, t, :, :, cells] = jnp.where(low_half3, pltpu.roll(left, 64, 2), right)
            left, right = lower[j, 0], lower[j, 1]
            heavy[2, t, :, :, cells] = jnp.where(low_half3, left, pltpu.roll(right, 64, 2))
    column = lax.broadcasted_iota(jnp.int32, (16, 128), 0)
    sum_u = jnp.zeros((16, 128), F32)
    sum_a = jnp.zeros((16, 128), F32)
    for s in range(8):
        for other in range(2):
            hit = column == 5 * s // 4 + other
            sum_u = sum_u + jnp.where(hit, pltpu.roll(total[s], 64 - 16 * other, 1), 0.0)
            sum_a = sum_a + jnp.where(hit, pltpu.roll(total[s], 32 - 16 * other, 1), 0.0)
    lane = lax.broadcasted_iota(jnp.int32, (16, 128), 1)
    valid = (lane < ROWS) & (column < COLS)
    area = jnp.where(valid, sum_u[:, ROWS : ROWS + 1], 1.0)
    speed = sum_u / area
    reverse = sum_a / area
    coeff = jnp.where(valid, -thrust[...] * speed * (1.5 * speed + reverse), 0.0)
    cell = lax.broadcasted_iota(jnp.int32, (16, NY), 1)
    band = lax.broadcasted_iota(jnp.int32, (16, NY), 0)
    spread = jnp.where(cell * COLS // NY == band, 1.0, 0.0).astype(F32)
    exact = lax.Precision.HIGHEST
    per_column = lax.dot_general(
        row_basis[...], coeff, (((1,), (1,)), ((), ())), precision=exact, preferred_element_type=F32
    )
    forced[...] = jnp.dot(per_column, spread, precision=exact, preferred_element_type=F32)

    scale_x = [wave_x[c] for c in range(2)]
    scale_y = wave_y[0:1, :]

    def forward(block, carry):
        entries = []
        for i in range(4):
            z = 4 * block + i
            up = spectrum[2, z + 1] if z + 1 < NZ else 0.0
            down = spectrum[2, z - 1] if z > 0 else 0.0
            entries.append(
                signed_x(spectrum[0, z], scale_x)
                + signed_y(spectrum[1, z], scale_y)
                + 0.5 * (up - down)
            )
        entries[0] = entries[0] - carry
        last = None
        for i in range(4):
            halves = []
            for q in range(2):
                cells = slice(256 * q, 256 * q + 256)
                total = inverses[block, 4 * i] * entries[0][:, cells]
                for j in range(1, 4):
                    total = total + inverses[block, 4 * i + j] * entries[j][:, cells]
                halves.append(total)
            last = jnp.concatenate(halves, axis=1)
            solved[4 * block + i] = last
        return last

    parts = [[(component, group) for component in range(3)] for group in range(4)]
    carry = jnp.zeros((16, NY), F32)
    fetch[0].wait()
    place(0, parts[0])
    fetch_tables.wait()
    for group in range(4):
        if group < 3:
            fetch[group + 1].wait()
        if group == 1:
            fetch_inverses.wait()
        multiply(group, parts[group])
        if group < 3:
            place(group + 1, parts[group + 1])
        if group > 0:
            for block in range(max(3 * group - 4, 0), 3 * group - 1):
                carry = forward(block, carry)
    for block in range(8, BLOCKS):
        carry = forward(block, carry)

    def corrected(block, i, running):
        column = inverses[block, 4 * i + 3]
        return solved[4 * block + i] - jnp.concatenate([column, column], axis=1) * running

    def write(group):
        return pltpu.make_async_copy(
            staged.at[group], out.at[:, :, pl.ds(pl.multiple_of(8 * group, 8), 8), :], sems.at[group]
        )

    def backward(step, upper):
        group = 5 - step
        first = 2 * group
        running = upper
        pressure = [None] * 8
        for half in (1, 0):
            for i in range(4):
                pressure[4 * half + i] = corrected(first + half, i, running)
            running = pressure[4 * half]
        before = corrected(jnp.maximum(first - 1, 0), 3, running)
        before = jnp.where(group > 0, before, 0.0)
        pressure = [before] + pressure + [upper]
        for component in range(3):
            for z in range(8):
                here = pressure[z + 1]
                if component == 0:
                    slope = signed_x(here, scale_x)
                elif component == 1:
                    slope = signed_y(here, scale_y)
                else:
                    slope = 0.5 * (pressure[z + 2] - pressure[z])
                value = spectrum[component, 8 * group + z] - slope
                for j in range(4):
                    turned[component, j, pl.ds(16 * z, 16), :] = value[:, 128 * j : 128 * j + 128]
            for r in range(16):
                sine, slot, inner = (r // 4) % 2, (r // 2) % 2, r % 2
                if r < 8:
                    mode = 4 * (2 * inner + (slot ^ parity[0])) + sine
                else:
                    mode = 4 * (r % 4) + 2 + sine
                for j in range(4):
                    cells = pl.ds(128 * j, 128)
                    staged[group, component, mode, :, cells] = turned[component, j, pl.ds(r, 8, stride=16), :]
        write(group).start()
        return running

    lax.fori_loop(0, 6, backward, jnp.zeros((16, NY), F32))
    for group in range(6):
        write(group).wait()


def across(parity, received, thrust, row_basis, wave_x, wave_y, inverses):
    tables = across_tables()
    smem = pl.BlockSpec(memory_space=pltpu.SMEM)
    vmem = pl.BlockSpec(memory_space=pltpu.VMEM)
    hbm = pl.BlockSpec(memory_space=pltpu.HBM)
    return pl.pallas_call(
        across_kernel,
        out_shape=jax.ShapeDtypeStruct((3, 16, NZ, NY), F32),
        in_specs=[smem] + [vmem] * 4 + [hbm] * 3,
        out_specs=hbm,
        scratch_shapes=[
            pltpu.VMEM((8, 4, GROUP, 128), F32),
            pltpu.VMEM((4, 8, 4, 8, 128), F32),
            pltpu.VMEM((BLOCKS, 16, 16, 256), F32),
            pltpu.VMEM((2, NY, NY), BF16),
            pltpu.VMEM((3, NZ, 16, NY), F32),
            pltpu.VMEM((NZ, 16, NY), F32),
            pltpu.VMEM((576, NY), BF16),
            pltpu.VMEM((576, NY), BF16),
            pltpu.VMEM((576, NY), BF16),
            pltpu.VMEM((576, NY), BF16),
            pltpu.VMEM((16, NY), F32),
            pltpu.VMEM((3, 4, 4, 1, NY), F32),
            pltpu.VMEM((3, 4, 128, 128), F32),
            pltpu.VMEM((6, 3, 16, 8, NY), F32),
            pltpu.SemaphoreType.DMA((16,)),
        ],
        compiler_params=pltpu.CompilerParams(vmem_limit_bytes=VMEM_BYTES),
        name="across",
    )(parity, thrust, row_basis, wave_x, wave_y, received, inverses, jnp.asarray(tables))


def body(adjoint, saved_grad, saved_u, disk_owner, disk_weight, row_x, thrust, block_inverse):
    axes = ("span", "stream")
    span = lax.axis_index("span")
    first_column = (5 * span // 4).astype(jnp.int32).reshape(1)
    sent = along(adjoint, saved_grad, saved_u, disk_owner, disk_weight, row_x, first_column)
    received = lax.all_to_all(
        sent.reshape(DESTS, 1, ROWS_SENT * 128), axes, split_axis=0, concat_axis=0, tiled=True
    ).reshape(8, 4, GROUP, 128)

    device = lax.axis_index(axes).astype(jnp.int32)
    parity = device % 2
    row = jnp.arange(16, dtype=jnp.int32)
    sine, slot, inner = (row // 4) % 2, (row // 2) % 2, row % 2
    local = jnp.where(row < 8, 4 * inner + 2 * (slot ^ parity), 2 * (row % 4) + 1)
    mode = 8 * device + local
    wave = 2.0 * math.pi * mode.astype(F32) / NX
    wave_x = jnp.where(sine == 0, wave, -wave).reshape(2, 8, 1)
    wave_y = (2.0 * math.pi * jnp.arange(NY // 2, dtype=F32) / NY).reshape(1, 256)
    angle = (mode[:, None] * row_x[None, :] % NX).astype(F32) * (2.0 * math.pi / NX)
    basis = jnp.where(sine[:, None] == 0, jnp.cos(angle), jnp.sin(angle)) / math.sqrt(NX)
    row_basis = jnp.pad(basis, ((0, 0), (0, 128 - ROWS)))
    thrust_t = jnp.pad(thrust.T, ((0, 16 - COLS), (0, 128 - ROWS)))
    folded = block_inverse.reshape(2, 2, 2, BLOCKS, 16, 256)
    even = folded[:, :, 0].transpose(2, 3, 1, 0, 4)
    even = jnp.where(parity == 0, even, even[:, :, ::-1]).reshape(BLOCKS, 16, 1, 4, 256)
    odd = folded[:, :, 1].transpose(2, 3, 0, 1, 4).reshape(BLOCKS, 16, 1, 4, 256)
    inverses = jnp.concatenate([even, even, odd, odd], axis=2).reshape(BLOCKS, 16, 16, 256)
    return across(
        parity.reshape(1), received, thrust_t, row_basis, wave_x, wave_y, inverses
    )


def solution(mesh):
    in_specs = (
        P(None, "stream", "span", None),
        P(None, "stream", "span", None),
        P("stream", "span", None),
        P("stream", "span"),
        P("stream", "span"),
        P(),
        P(),
        P(("span", "stream"), None, None, None, None),
    )
    out_specs = P(None, ("span", "stream"), None, None)
    return jax.shard_map(body, mesh=mesh, in_specs=in_specs, out_specs=out_specs, check_vma=False)
```

```python
import functools
import math

import jax
import jax.numpy as jnp
import ml_dtypes
import numpy as np
from jax import lax
from jax.experimental import pallas as pl
from jax.experimental.pallas import tpu as pltpu
from jax.sharding import PartitionSpec as P

NX = 2048
NY = 512
NZ = 48
ROWS = 10
COLS = 10
HALF = NX // 2
BLOCKS = NZ // 4
DESTS = 128
ROWS_SENT = 74
GROUP = 4 * ROWS_SENT
F32 = jnp.float32
BF16 = jnp.bfloat16
VMEM_BYTES = 58 * 1024 * 1024


def split_table(values):
    high = values.astype(ml_dtypes.bfloat16)
    low = (values - high.astype(np.float64)).astype(ml_dtypes.bfloat16)
    return high, low


def wave_rows(mode, sine, length):
    phase = mode[:, None] * np.arange(length)[None, :] % NX
    angle = phase * (2.0 * np.pi / NX)
    return np.where(sine[:, None] == 0, np.cos(angle), np.sin(angle)) / np.sqrt(NX)


@functools.lru_cache(maxsize=None)
def along_tables():
    row = np.arange(HALF)
    sine, rest = (row // 4) % 2, row % 4
    odd = wave_rows(8 * (row // 8) + 2 * rest + 1, sine, HALF)
    row = np.arange(HALF // 2)
    sine, slot, inner = (row // 4) % 2, (row // 2) % 2, row % 2
    even = [
        wave_rows(8 * (2 * (row // 8) + (slot ^ kind)) + 4 * inner + 2 * kind, sine, HALF // 2)
        for kind in range(2)
    ]
    odd = np.stack(split_table(odd)).transpose(0, 2, 1).reshape(2, HALF, 2, HALF // 2)
    even = np.stack(split_table(np.stack(even))).transpose(1, 0, 3, 2)
    even = even.reshape(2, 2, HALF // 2, 2, HALF // 4)
    return odd.transpose(2, 0, 1, 3), even.transpose(3, 0, 1, 2, 4)


@functools.lru_cache(maxsize=None)
def across_tables():
    basis = np.arange(NY)
    phase = np.arange(NY)[:, None] * (basis % (NY // 2))[None, :] % NY
    angle = phase * (2.0 * np.pi / NY)
    values = np.where((basis // (NY // 2))[None, :] == 0, np.cos(angle), np.sin(angle))
    return np.stack(split_table(values / np.sqrt(NY)))


def split(value):
    high = value.astype(BF16)
    return high, (value - high.astype(F32)).astype(BF16)


def dot_nt(left, right):
    return lax.dot_general(left, right, (((1,), (1,)), ((), ())), preferred_element_type=F32)


def dot_nn(left, right):
    return jnp.dot(left, right, preferred_element_type=F32)


def couple(level, step, adjoint, grad, source_high, source_low):
    quarter = NX // 4
    rows = pl.ds(pl.multiple_of(16 * step, 16), 16)
    for start in range(0, quarter, 128):
        lanes = [pl.ds(quarter * n + start, 128) for n in range(4)]
        velocity = [[adjoint[j, level, rows, l].astype(F32) for l in lanes] for j in range(3)]
        for i in range(3):
            value = []
            for n, l in enumerate(lanes):
                total = velocity[0][n] * grad[3 * i, level, rows, l].astype(F32)
                for j in range(1, 3):
                    total = total + velocity[j][n] * grad[3 * i + j, level, rows, l].astype(F32)
                value.append(total)
            first, second = value[0] + value[2], value[1] + value[3]
            folded = (value[0] - value[2], value[1] - value[3], first + second, first - second)
            target = pl.ds(pl.multiple_of(64 * (3 * level + i) + 16 * step, 16), 16)
            for n in range(4):
                high, low = split(folded[n])
                source_high[target, lanes[n]] = high
                source_low[target, lanes[n]] = low


def along_kernel(
    row_x, first_column, owner, weight, adjoint_hbm, grad_hbm, saved_u_hbm, odd_hbm, even_hbm,
    out, adjoint, grad, saved_u, odd, even, source_high, source_low, onehot, outbox, sems,
):
    copies = []
    for level in range(3):
        copies.append(pltpu.make_async_copy(adjoint_hbm.at[:, level], adjoint.at[:, level], sems.at[2 * level]))
        copies.append(pltpu.make_async_copy(grad_hbm.at[:, level], grad.at[:, level], sems.at[2 * level + 1]))
    fetch_u = pltpu.make_async_copy(saved_u_hbm, saved_u, sems.at[6])

    def fetch_tables(step):
        return (
            pltpu.make_async_copy(odd_hbm.at[step], odd.at[step], sems.at[7 + 2 * step]),
            pltpu.make_async_copy(even_hbm.at[step], even.at[step], sems.at[8 + 2 * step]),
        )

    early, late = fetch_tables(0), fetch_tables(1)
    for copy in copies + [fetch_u] + list(early) + list(late):
        copy.start()

    lane = lax.broadcasted_iota(jnp.int32, (1, 128), 1) % 16
    wanted = jnp.full((1, 128), -1, jnp.int32)
    for r in range(ROWS):
        wanted = jnp.where(lane == r, row_x[r], wanted)

    def mark(step, _):
        rows = pl.ds(pl.multiple_of(256 * step, 256), 256)
        cell = lax.broadcasted_iota(jnp.int32, (256, 128), 0) + 256 * step
        onehot[rows, :] = jnp.where(cell == wanted, 1.0, 0.0).astype(BF16)
        return 0

    lax.fori_loop(0, NX // 256, mark, 0)

    def couple_rows(level):
        def rows_of(step, _):
            couple(level, step, adjoint, grad, source_high, source_low)
            return 0

        lax.fori_loop(0, 4, rows_of, 0)

    sums_u, sums_a, masked = [], [], []

    def disk_level(level):
        column_u = dot_nn(saved_u[level], onehot[...])
        column_a = dot_nn(adjoint[0, level], onehot[...]).astype(BF16)
        column_u = jnp.where(lane == ROWS, 1.0, column_u).astype(BF16)
        own = owner[level : level + 1, :]
        heavy = weight[level : level + 1, :]
        masked.append(jnp.where(own >= 0, heavy, 0.0))
        row = lax.broadcasted_iota(jnp.int32, (8, 64), 0)
        rest = jnp.where(own == first_column[0] + row % 2, heavy, 0.0)
        for _ in range(3):
            part = rest.astype(BF16)
            rest = rest - part.astype(F32)
            sums_u.append(dot_nn(part, column_u))
            sums_a.append(dot_nn(part, column_a))

    def disk_rows():
        sum_u = functools.reduce(jnp.add, sums_u)
        sum_a = functools.reduce(jnp.add, sums_a)
        place = lax.broadcasted_iota(jnp.int32, (1, 128), 1) // 16
        sums = jnp.where(place == 4, sum_u[0:1], sum_u[1:2])
        sums = jnp.where(place == 6, sum_a[0:1], jnp.where(place == 7, sum_a[1:2], sums))
        last = jnp.concatenate([masked[2], jnp.zeros((1, 64), F32)], axis=1)
        last = jnp.where(place < 4, last, sums)
        return jnp.concatenate([jnp.concatenate(masked[:2], axis=1), last], axis=0)

    first_slot = lax.broadcasted_iota(jnp.int32, (8, 128), 0) % 4 < 2
    low_half = lax.broadcasted_iota(jnp.int32, (8, 128), 1) < 64

    def product(rows, span, high, low):
        cells = pl.ds(span, high.shape[0])
        result = dot_nn(source_high[rows, cells], high)
        result = result + dot_nn(source_low[rows, cells], high)
        return result + dot_nn(source_high[rows, cells], low)

    def send(step, block):
        part = pl.ds(16 * step + 8 * block, 8)
        return pltpu.make_async_copy(outbox.at[part], out.at[part], sems.at[11 + 2 * step + block])

    def fill(step, start, count, tiles, extra=None):
        rows = pl.ds(start, count)

        def turned(value, tile, block):
            lanes = slice(128 * block, 128 * block + 128)
            begin = 128 * tile - start
            if tile < 4:
                part = value[begin : begin + 128, lanes]
            else:
                part = jnp.concatenate([value[begin : begin + 64, lanes]] * 2, axis=0)
            return part.T

        def store(dest, tile, value):
            place = ROWS_SENT * (dest % 4) + 8 * tile
            outbox[16 * step + dest // 4, pl.ds(place, 8), :] = value

        kinds = [
            product(rows, HALF + HALF // 2 * k, even[step, k, 0], even[step, k, 1]) for k in range(2)
        ]
        for block in range(2):
            modes = pl.ds(256 * block, 256)
            rest = product(rows, 0, odd[step, 0, :, modes], odd[step, 1, :, modes])
            for tile in tiles:
                pair = [turned(value, tile, block) for value in kinds]
                for side in range(2):
                    single = turned(rest, tile, side)
                    for index in range(16):
                        dest = 32 * block + 16 * side + index
                        part = slice(8 * (dest // 2 % 16), 8 * (dest // 2 % 16) + 8)
                        even_part = jnp.where(first_slot, pair[dest % 2][part], pair[1 - dest % 2][part])
                        odd_part = single[8 * index : 8 * index + 8]
                        if tile < 4:
                            store(dest, tile, even_part)
                            store(dest, 4 + tile, odd_part)
                        else:
                            store(dest, 8, jnp.where(low_half, even_part, odd_part))
            if extra is not None:
                for dest in range(32 * block, 32 * block + 32):
                    outbox[16 * step + dest // 4, pl.ds(ROWS_SENT * (dest % 4) + 72, 2), :] = extra
                send(step, block).start()

    def wait_for(level):
        copies[2 * level].wait()
        copies[2 * level + 1].wait()

    wait_for(0)
    couple_rows(0)
    wait_for(1)
    couple_rows(1)
    fetch_u.wait()
    disk_level(0)
    disk_level(1)
    wait_for(2)
    for copy in early:
        copy.wait()
    for step in range(4):
        couple(2, step, adjoint, grad, source_high, source_low)
    disk_level(2)
    extra = disk_rows()
    fill(0, 0, 384, range(3))
    fill(0, 384, 192, range(3, 5), extra)
    for copy in late:
        copy.wait()
    fill(1, 0, 576, range(5), extra)
    for step in range(2):
        for block in range(2):
            send(step, block).wait()


def along(adjoint, grad, saved_u, owner, weight, row_x, first_column):
    odd, even = along_tables()
    smem = pl.BlockSpec(memory_space=pltpu.SMEM)
    vmem = pl.BlockSpec(memory_space=pltpu.VMEM)
    hbm = pl.BlockSpec(memory_space=pltpu.HBM)
    return pl.pallas_call(
        along_kernel,
        out_shape=jax.ShapeDtypeStruct((DESTS // 4, GROUP, 128), F32),
        in_specs=[smem, smem, vmem, vmem, hbm, hbm, hbm, hbm, hbm],
        out_specs=hbm,
        scratch_shapes=[
            pltpu.VMEM((3, 3, 64, NX), BF16),
            pltpu.VMEM((9, 3, 64, NX), BF16),
            pltpu.VMEM((3, 64, NX), BF16),
            pltpu.VMEM(odd.shape, BF16),
            pltpu.VMEM(even.shape, BF16),
            pltpu.VMEM((576, NX), BF16),
            pltpu.VMEM((576, NX), BF16),
            pltpu.VMEM((NX, 128), BF16),
            pltpu.VMEM((DESTS // 4, GROUP, 128), F32),
            pltpu.SemaphoreType.DMA((15,)),
        ],
        compiler_params=pltpu.CompilerParams(vmem_limit_bytes=VMEM_BYTES),
        name="along",
    )(row_x, first_column, owner, weight, adjoint, grad, saved_u, jnp.asarray(odd), jnp.asarray(even))


def signed_x(value, scale):
    return jnp.concatenate(
        [scale[c] * pltpu.roll(value[8 * c : 8 * c + 8], 4, 0) for c in range(2)], axis=0
    )


def signed_y(value, scale):
    return jnp.concatenate([scale * value[:, 256:], -scale * value[:, :256]], axis=1)


def across_kernel(
    parity, thrust, row_basis, wave_x, wave_y, received_hbm, inverses_hbm, tables_hbm,
    out, received, extras, inverses, tables, spectrum, solved, high_0, high_1, low_0, low_1, forced, heavy, turned, staged, sems,
):
    fetch_extras = []
    for t in range(4):
        window = pl.ds((ROWS_SENT * t + 72) // 8 * 8, 8)
        fetch_extras.append(
            pltpu.make_async_copy(received_hbm.at[:, :, window], extras.at[t], sems.at[12 + t])
        )
    fetch = [
        pltpu.make_async_copy(received_hbm.at[:, group], received.at[:, group], sems.at[6 + group])
        for group in range(4)
    ]
    fetch_tables = pltpu.make_async_copy(tables_hbm, tables, sems.at[10])
    fetch_inverses = pltpu.make_async_copy(inverses_hbm, inverses, sems.at[11])
    for copy in fetch_extras + [fetch[0], fetch_tables, fetch[1], fetch_inverses] + fetch[2:]:
        copy.start()
    grids = ((high_0, low_0), (high_1, low_1))
    low_half = lax.broadcasted_iota(jnp.int32, (1, 128), 1) < 64
    low_half3 = low_half[None]

    def place(unit, parts):
        high_grid, low_grid = grids[unit % 2]
        for n, (component, group) in enumerate(parts):
            for t in range(4):
                for inner in range(3):
                    pair = 3 * inner + component
                    target = pl.ds(192 * n + 16 * (3 * t + inner), 16)
                    for j in range(4):
                        cells = pl.ds(128 * j, 128)
                        values = []
                        for kind in range(2):
                            tile, side = (4 * kind + pair // 2, pair % 2) if pair < 8 else (8, kind)
                            rows = pl.ds(ROWS_SENT * t + 8 * tile, 8)
                            left = received[2 * j, group, rows, :]
                            right = received[2 * j + 1, group, rows, :]
                            if side == 0:
                                value = jnp.where(low_half, left, pltpu.roll(right, 64, 1))
                            else:
                                value = jnp.where(low_half, pltpu.roll(left, 64, 1), right)
                            if component == 0:
                                disk = heavy[inner, t, group, :, cells]
                                value = value + disk * forced[pl.ds(8 * kind, 8), cells]
                            values.append(value)
                        high, low = split(jnp.concatenate(values, axis=0))
                        high_grid[target, cells] = high
                        low_grid[target, cells] = low

    def multiply(unit, parts):
        high_grid, low_grid = grids[unit % 2]
        result = dot_nn(high_grid[...], tables[0])
        result = result + dot_nn(low_grid[...], tables[0])
        result = result + dot_nn(high_grid[...], tables[1])
        for n, (component, group) in enumerate(parts):
            spectrum[component, pl.ds(12 * group, 12)] = result[192 * n : 192 * n + 192].reshape(12, 16, NY)

    for copy in fetch_extras:
        copy.wait()
    total = jnp.zeros((8, 1, 128), F32)
    for t in range(4):
        start = (ROWS_SENT * t + 72) % 8
        upper = extras[t, :, :, pl.ds(start, 1), :].reshape(4, 2, 4, 1, 128)
        lower = extras[t, :, :, pl.ds(start + 1, 1), :]
        total = total + jnp.sum(lower, axis=1)
        lower = lower.reshape(4, 2, 4, 1, 128)
        for j in range(4):
            cells = pl.ds(128 * j, 128)
            left, right = upper[j, 0], upper[j, 1]
            heavy[0, t, :, :, cells] = jnp.where(low_half3, left, pltpu.roll(right, 64, 2))
            heavy[1, t, :, :, cells] = jnp.where(low_half3, pltpu.roll(left, 64, 2), right)
            left, right = lower[j, 0], lower[j, 1]
            heavy[2, t, :, :, cells] = jnp.where(low_half3, left, pltpu.roll(right, 64, 2))
    column = lax.broadcasted_iota(jnp.int32, (16, 128), 0)
    sum_u = jnp.zeros((16, 128), F32)
    sum_a = jnp.zeros((16, 128), F32)
    for s in range(8):
        for other in range(2):
            hit = column == 5 * s // 4 + other
            sum_u = sum_u + jnp.where(hit, pltpu.roll(total[s], 64 - 16 * other, 1), 0.0)
            sum_a = sum_a + jnp.where(hit, pltpu.roll(total[s], 32 - 16 * other, 1), 0.0)
    lane = lax.broadcasted_iota(jnp.int32, (16, 128), 1)
    valid = (lane < ROWS) & (column < COLS)
    area = jnp.where(valid, sum_u[:, ROWS : ROWS + 1], 1.0)
    speed = sum_u / area
    reverse = sum_a / area
    coeff = jnp.where(valid, -thrust[...] * speed * (1.5 * speed + reverse), 0.0)
    cell = lax.broadcasted_iota(jnp.int32, (16, NY), 1)
    band = lax.broadcasted_iota(jnp.int32, (16, NY), 0)
    spread = jnp.where(cell * COLS // NY == band, 1.0, 0.0).astype(F32)
    exact = lax.Precision.HIGHEST
    per_column = lax.dot_general(
        row_basis[...], coeff, (((1,), (1,)), ((), ())), precision=exact, preferred_element_type=F32
    )
    forced[...] = jnp.dot(per_column, spread, precision=exact, preferred_element_type=F32)

    scale_x = [wave_x[c] for c in range(2)]
    scale_y = wave_y[0:1, :]

    def forward(block, carry):
        entries = []
        for i in range(4):
            z = 4 * block + i
            up = spectrum[2, z + 1] if z + 1 < NZ else 0.0
            down = spectrum[2, z - 1] if z > 0 else 0.0
            entries.append(
                signed_x(spectrum[0, z], scale_x)
                + signed_y(spectrum[1, z], scale_y)
                + 0.5 * (up - down)
            )
        entries[0] = entries[0] - carry
        last = None
        for i in range(4):
            halves = []
            for q in range(2):
                cells = slice(256 * q, 256 * q + 256)
                total = inverses[block, 4 * i] * entries[0][:, cells]
                for j in range(1, 4):
                    total = total + inverses[block, 4 * i + j] * entries[j][:, cells]
                halves.append(total)
            last = jnp.concatenate(halves, axis=1)
            solved[4 * block + i] = last
        return last

    parts = [[(component, group) for component in range(3)] for group in range(4)]
    carry = jnp.zeros((16, NY), F32)
    fetch[0].wait()
    place(0, parts[0])
    fetch_tables.wait()
    for group in range(4):
        if group < 3:
            fetch[group + 1].wait()
        if group == 1:
            fetch_inverses.wait()
        multiply(group, parts[group])
        if group < 3:
            place(group + 1, parts[group + 1])
        if group > 0:
            for block in range(max(3 * group - 4, 0), 3 * group - 1):
                carry = forward(block, carry)
    for block in range(8, BLOCKS):
        carry = forward(block, carry)

    def corrected(block, i, running):
        column = inverses[block, 4 * i + 3]
        return solved[4 * block + i] - jnp.concatenate([column, column], axis=1) * running

    def write(group, component):
        return pltpu.make_async_copy(
            staged.at[group, component],
            out.at[component, :, pl.ds(pl.multiple_of(8 * group, 8), 8), :],
            sems.at[16 + 3 * group + component],
        )

    def backward(step, upper):
        group = 5 - step
        first = 2 * group
        running = upper
        pressure = [None] * 8
        for half in (1, 0):
            for i in range(4):
                pressure[4 * half + i] = corrected(first + half, i, running)
            running = pressure[4 * half]
        before = corrected(jnp.maximum(first - 1, 0), 3, running)
        before = jnp.where(group > 0, before, 0.0)
        pressure = [before] + pressure + [upper]
        for component in range(3):
            for z in range(8):
                here = pressure[z + 1]
                if component == 0:
                    slope = signed_x(here, scale_x)
                elif component == 1:
                    slope = signed_y(here, scale_y)
                else:
                    slope = 0.5 * (pressure[z + 2] - pressure[z])
                value = spectrum[component, 8 * group + z] - slope
                for j in range(4):
                    turned[component, j, pl.ds(16 * z, 16), :] = value[:, 128 * j : 128 * j + 128]
            for r in range(16):
                sine, slot, inner = (r // 4) % 2, (r // 2) % 2, r % 2
                if r < 8:
                    mode = 4 * (2 * inner + (slot ^ parity[0])) + sine
                else:
                    mode = 4 * (r % 4) + 2 + sine
                for j in range(4):
                    cells = pl.ds(128 * j, 128)
                    staged[group, component, mode, :, cells] = turned[component, j, pl.ds(r, 8, stride=16), :]
            write(group, component).start()
        return running

    lax.fori_loop(0, 6, backward, jnp.zeros((16, NY), F32))
    for group in range(6):
        for component in range(3):
            write(group, component).wait()


def across(parity, received, thrust, row_basis, wave_x, wave_y, inverses):
    tables = across_tables()
    smem = pl.BlockSpec(memory_space=pltpu.SMEM)
    vmem = pl.BlockSpec(memory_space=pltpu.VMEM)
    hbm = pl.BlockSpec(memory_space=pltpu.HBM)
    return pl.pallas_call(
        across_kernel,
        out_shape=jax.ShapeDtypeStruct((3, 16, NZ, NY), F32),
        in_specs=[smem] + [vmem] * 4 + [hbm] * 3,
        out_specs=hbm,
        scratch_shapes=[
            pltpu.VMEM((8, 4, GROUP, 128), F32),
            pltpu.VMEM((4, 8, 4, 8, 128), F32),
            pltpu.VMEM((BLOCKS, 16, 16, 256), F32),
            pltpu.VMEM((2, NY, NY), BF16),
            pltpu.VMEM((3, NZ, 16, NY), F32),
            pltpu.VMEM((NZ, 16, NY), F32),
            pltpu.VMEM((576, NY), BF16),
            pltpu.VMEM((576, NY), BF16),
            pltpu.VMEM((576, NY), BF16),
            pltpu.VMEM((576, NY), BF16),
            pltpu.VMEM((16, NY), F32),
            pltpu.VMEM((3, 4, 4, 1, NY), F32),
            pltpu.VMEM((3, 4, 128, 128), F32),
            pltpu.VMEM((6, 3, 16, 8, NY), F32),
            pltpu.SemaphoreType.DMA((34,)),
        ],
        compiler_params=pltpu.CompilerParams(vmem_limit_bytes=VMEM_BYTES),
        name="across",
    )(parity, thrust, row_basis, wave_x, wave_y, received, inverses, jnp.asarray(tables))


def body(adjoint, saved_grad, saved_u, disk_owner, disk_weight, row_x, thrust, block_inverse):
    axes = ("span", "stream")
    span = lax.axis_index("span")
    first_column = (5 * span // 4).astype(jnp.int32).reshape(1)
    sent = along(adjoint, saved_grad, saved_u, disk_owner, disk_weight, row_x, first_column)
    received = lax.all_to_all(
        sent.reshape(DESTS, 1, ROWS_SENT * 128), axes, split_axis=0, concat_axis=0, tiled=True
    ).reshape(8, 4, GROUP, 128)

    device = lax.axis_index(axes).astype(jnp.int32)
    parity = device % 2
    row = jnp.arange(16, dtype=jnp.int32)
    sine, slot, inner = (row // 4) % 2, (row // 2) % 2, row % 2
    local = jnp.where(row < 8, 4 * inner + 2 * (slot ^ parity), 2 * (row % 4) + 1)
    mode = 8 * device + local
    wave = 2.0 * math.pi * mode.astype(F32) / NX
    wave_x = jnp.where(sine == 0, wave, -wave).reshape(2, 8, 1)
    wave_y = (2.0 * math.pi * jnp.arange(NY // 2, dtype=F32) / NY).reshape(1, 256)
    angle = (mode[:, None] * row_x[None, :] % NX).astype(F32) * (2.0 * math.pi / NX)
    basis = jnp.where(sine[:, None] == 0, jnp.cos(angle), jnp.sin(angle)) / math.sqrt(NX)
    row_basis = jnp.pad(basis, ((0, 0), (0, 128 - ROWS)))
    thrust_t = jnp.pad(thrust.T, ((0, 16 - COLS), (0, 128 - ROWS)))
    folded = block_inverse.reshape(2, 2, 2, BLOCKS, 16, 256)
    even = folded[:, :, 0].transpose(2, 3, 1, 0, 4)
    even = jnp.where(parity == 0, even, even[:, :, ::-1]).reshape(BLOCKS, 16, 1, 4, 256)
    odd = folded[:, :, 1].transpose(2, 3, 0, 1, 4).reshape(BLOCKS, 16, 1, 4, 256)
    inverses = jnp.concatenate([even, even, odd, odd], axis=2).reshape(BLOCKS, 16, 16, 256)
    return across(
        parity.reshape(1), received, thrust_t, row_basis, wave_x, wave_y, inverses
    )


def solution(mesh):
    in_specs = (
        P(None, "stream", "span", None),
        P(None, "stream", "span", None),
        P("stream", "span", None),
        P("stream", "span"),
        P("stream", "span"),
        P(),
        P(),
        P(("span", "stream"), None, None, None, None),
    )
    out_specs = P(None, ("span", "stream"), None, None)
    return jax.shard_map(body, mesh=mesh, in_specs=in_specs, out_specs=out_specs, check_vma=False)
```
